32 devices in a mesh: dp: 2 (over x), section: 4 (over z), tm: 4 (over y, core).
Axes of the slice: x: 2, y: 2, z: 4, core: 2. Of those that a mesh axis runs over, the one named last changes fastest.
Arguments:
- frames: bfloat16 [4, 512, 1280], P('dp', 'tm'), may hold values from -6 to 6
- block_mask: int32 [4, 8, 2], P('dp', 'tm'), may hold values 0 or 1
- span_segment: int32 [4, 8], P('dp'), may hold values from 0 to 3, as said below
- dec_states: bfloat16 [512, 1280], P(('dp', 'tm')), may hold values from -6 to 6
- enc_qkv: bfloat16 [4, 1280, 1920], P('section', ('dp', 'tm')), may hold values from -0.15625 to 0.15625
- enc_out: bfloat16 [4, 640, 1280], P('section', None, ('dp', 'tm')), may hold values from -0.75 to 0.75
- cross_query: bfloat16 [1280, 768], P(('dp', 'tm'), 'section'), may hold values from -0.15625 to 0.15625
- cross_key: bfloat16 [1280, 768], P(('dp', 'tm'), 'section'), may hold values from -0.15625 to 0.15625
- cross_value: bfloat16 [1280, 768], P(('dp', 'tm'), 'section'), may hold values from -0.75 to 0.75
- cotangent: bfloat16 [512, 1280], P(('dp', 'tm')), may hold values from -1.5 to 1.5
Outputs:
- context: bfloat16 [512, 768], P(('dp', 'tm'), 'section')
- out_grad: float32 [768, 1280], P('section', ('dp', 'tm'))
The draws below stay inside these ranges and needn't reach their ends.
Inputs may be any that keep to these rules, and one draw needn't show every extreme that they name: `span_segment`: the first of every 2 blocks, block d * 2, serves segment (d + 2) mod 4; every other block serves a segment drawn evenly.
All inputs are finite; a program needn't handle non-finite values. No bound on the sum of `block_mask` on one device may be relied on, other than what follows from the above.
Results may differ from the reference program's by a relative error of at most 0.011.
Values may be sent and summed in bfloat16 or wider, within the bound.
A program may use at most 64 MiB of HBM per device.

```python
import jax
import jax.numpy as jnp
from jax import lax

D = 1280
HD = 64
ENC_HEADS = 10
BLK = 64
MB = 2
TF = 128
DTOK = 32
SEQS = 4
FRAMES = 512
NBLK = 8
CROSS_HEADS = 12
TOKALL = 512
N_DP = 2
N_SECTION = 4
N_TM = 4


def draw_span_segment(key, part):
    drawn = jax.random.randint(key, (SEQS, NBLK), 0, N_TM, dtype=jnp.int32)
    block_index = jnp.arange(NBLK, dtype=jnp.int32)
    per_shard = TF // BLK
    shard_of = block_index // per_shard
    leading = block_index % per_shard == 0
    opposite = (shard_of + N_TM // 2) % N_TM
    return jnp.where(leading[None, :], opposite[None, :], drawn).astype(jnp.int32)


def set_ends(values, stream_key, least, top_value):
    longest = values.shape.index(max(values.shape))
    spots = []
    for shift in (0, 1):
        where = [jax.random.randint(jax.random.fold_in(stream_key, axis), (), 0, length) for axis, length in enumerate(values.shape)]
        where[longest] = (where[longest] + shift) % values.shape[longest]
        spots.append(tuple(where))
    return values.at[spots[0]].set(least).at[spots[1]].set(top_value)


def strengthened(entries, own_key, source, target, shards_of, factor):
    def block_of(dim):
        return (jnp.arange(entries.shape[dim]) // (entries.shape[dim] // shards_of)).reshape((-1,) + (1,) * (entries.ndim - 1 - dim))

    one_side = jax.random.permutation(own_key, shards_of)[block_of(target)]
    other_side = (block_of(target) + shards_of // 2) % shards_of
    return jnp.where((block_of(source) == one_side) | (block_of(source) == other_side), factor * entries, entries)


def block_levels(stream_key, shape, shards, smallest, top_value):
    gain, own = 1.0, jax.random.fold_in(stream_key, 6)
    for position, blocks in shards:
        heights = jnp.exp(jax.random.uniform(jax.random.fold_in(own, position), (blocks,), jnp.float32, smallest / len(shards), top_value / len(shards)))
        gain = gain * jnp.repeat(heights, shape[position] // blocks).reshape([-1 if axis == position else 1 for axis in range(len(shape))])
    return gain


def bell_draw(stream_key, shape, width, limit, shards=(), held_as=jnp.bfloat16):
    loudness = block_levels(stream_key, shape, shards, -0.22, 0.18) if shards else 1.0
    values = jax.random.normal(stream_key, shape, jnp.float32) * width * loudness
    return jnp.minimum(jnp.maximum(values, -limit), limit).astype(held_as)


def heavy_noise(own_key, dims, scale, limit, cuts, heavy, kind=jnp.bfloat16):
    result = scale * jax.random.normal(own_key, dims, jnp.float32)
    if cuts:
        result = result * block_levels(own_key, dims, cuts, -0.22, 0.18)
    return jnp.clip(strengthened(result, jax.random.fold_in(own_key, 3), *heavy), -limit, limit).astype(kind)


def setup_inputs(seed: int = 0) -> dict:
    splits = jax.random.split(jax.random.key(seed), 11)
    return {
        "frames": bell_draw(splits[0], (SEQS, FRAMES, D), 1.0, 6.0, ((0, 2), (1, 4))),
        "block_mask": set_ends((jax.random.randint(splits[1], (SEQS, NBLK, 2), 0, 2) < 1).astype(jnp.int32), jax.random.fold_in(splits[1], 1), 0, 1),
        "span_segment": draw_span_segment(jax.random.fold_in(splits[10], 71), 0),
        "dec_states": bell_draw(splits[3], (TOKALL, D), 1.0, 6.0, ((0, 8),)),
        "enc_qkv": bell_draw(splits[4], (N_SECTION, D, 3 * ENC_HEADS * HD), D ** -0.5, 0.15625, ((0, 4), (1, 8))),
        "enc_out": bell_draw(splits[5], (N_SECTION, ENC_HEADS * HD, D), HD ** -0.5, 0.75, ((0, 4), (2, 8))),
        "cross_query": bell_draw(splits[6], (D, CROSS_HEADS * HD), D ** -0.5, 0.15625, ((0, 8), (1, 4))),
        "cross_key": bell_draw(splits[7], (D, CROSS_HEADS * HD), D ** -0.5, 0.15625, ((0, 8), (1, 4))),
        "cross_value": bell_draw(splits[8], (D, CROSS_HEADS * HD), HD ** -0.5, 0.75, ((0, 8), (1, 4))),
        "cotangent": heavy_noise(splits[9], (TOKALL, D), (4.0 * TOKALL ** -0.5), 1.5, ((0, 8),), (0, 1, 8, 2.0)),
    }


epsilon = 1e-05

def norm_rows(inputs):
    values32 = inputs.astype(jnp.float32)
    center = values32 - lax.optimization_barrier(jnp.mean(values32, axis=-1, keepdims=True))
    spread = lax.optimization_barrier(jnp.mean(center * center, axis=-1, keepdims=True))
    return (center * lax.rsqrt(spread + epsilon)).astype(jnp.bfloat16)

def allowed_keys(mask_rows, first_block, total_blocks):
    block_count = mask_rows.shape[0]
    block_index = first_block + jnp.arange(block_count, dtype=jnp.int32)
    left_open = (mask_rows[:, 0] == 1) & (block_index > 0)
    right_open = (mask_rows[:, 1] == 1) & (block_index < total_blocks - 1)
    middle = jnp.ones((block_count, BLK), dtype=jnp.bool_)
    return jnp.concatenate([jnp.broadcast_to(left_open[:, None], (block_count, BLK)), middle, jnp.broadcast_to(right_open[:, None], (block_count, BLK))], axis=1)

def window_attention(queries, key_rows, value_rows, allowed):
    frame_count = queries.shape[0]
    block_count = frame_count // BLK
    head_count = queries.shape[1] // HD

    def windows(padded):
        return jnp.concatenate([padded[offset * BLK:offset * BLK + frame_count].reshape(block_count, BLK, head_count, HD) for offset in range(3)], axis=1)
    query_blocks = queries.reshape(block_count, BLK, head_count, HD).astype(jnp.float32)
    scores = jnp.einsum('bqhd,bkhd->bhqk', query_blocks, windows(key_rows).astype(jnp.float32)) * HD ** (-0.5)
    weights = jnp.where(allowed[:, None, None, :], jnp.exp(scores), 0.0)
    totals = lax.optimization_barrier(jnp.sum(weights, axis=-1))
    summed = jnp.einsum('bhqk,bkhd->bqhd', weights.astype(jnp.bfloat16).astype(jnp.float32), windows(value_rows).astype(jnp.float32))
    context = summed / jnp.transpose(totals, (0, 2, 1))[..., None]
    return context.reshape(frame_count, head_count * HD).astype(jnp.bfloat16)

def encoder_layer(hidden, mask_rows, proj_qkv, proj_out):
    enc_width = proj_out.shape[0]
    normed = norm_rows(hidden)
    packed = jnp.dot(normed, proj_qkv, preferred_element_type=jnp.float32).astype(jnp.bfloat16)
    border = jnp.zeros((BLK, 2 * enc_width), jnp.bfloat16)
    key_value = jnp.concatenate([border, packed[:, enc_width:], border], axis=0)
    allowed = allowed_keys(mask_rows, 0, mask_rows.shape[0])
    context = window_attention(packed[:, :enc_width], key_value[:, :enc_width], key_value[:, enc_width:], allowed)
    update = jnp.dot(context, proj_out, preferred_element_type=jnp.float32)
    return (hidden.astype(jnp.float32) + update).astype(jnp.bfloat16)

def reference(frames, block_mask, span_segment, dec_states, enc_qkv, enc_out, cross_query, cross_key, cross_value, cotangent):

    def encode(operands):
        hidden, mask_rows = operands
        for section_layer in range(N_SECTION):
            hidden = encoder_layer(hidden, mask_rows, enc_qkv[section_layer], enc_out[section_layer])
        return hidden
    memory = lax.map(encode, (frames, block_mask))
    decoder = dec_states.reshape(N_DP, N_TM, MB, DTOK, D).transpose(0, 2, 1, 3, 4).reshape(SEQS, N_TM * DTOK, D)
    query_segment = jnp.arange(N_TM * DTOK, dtype=jnp.int32) // DTOK
    head_count = CROSS_HEADS

    def cross(operands):
        memory_rows, decoder_rows, segment_rows = operands
        mem_norm = norm_rows(memory_rows)
        key_rows = jnp.dot(mem_norm, cross_key, preferred_element_type=jnp.float32).astype(jnp.bfloat16)
        value_rows = jnp.dot(mem_norm, cross_value, preferred_element_type=jnp.float32).astype(jnp.bfloat16)
        query_rows = jnp.dot(norm_rows(decoder_rows), cross_query, preferred_element_type=jnp.float32).astype(jnp.bfloat16)
        frame_segment = jnp.repeat(segment_rows, BLK)
        allowed = query_segment[:, None] == frame_segment[None, :]

        def one_head(head_operands):
            head_query, head_key, head_value = head_operands
            scores = jnp.dot(head_query, head_key.T, preferred_element_type=jnp.float32) * HD ** (-0.5)
            weights = jnp.where(allowed, jnp.exp(scores), 0.0)
            totals = lax.optimization_barrier(jnp.sum(weights, axis=-1))
            summed = jnp.dot(weights.astype(jnp.bfloat16), head_value, preferred_element_type=jnp.float32)
            return summed / totals[:, None]
        split_query = query_rows.reshape(-1, head_count, HD).transpose(1, 0, 2)
        split_key = key_rows.reshape(-1, head_count, HD).transpose(1, 0, 2)
        split_value = value_rows.reshape(-1, head_count, HD).transpose(1, 0, 2)
        context = lax.map(one_head, (split_query, split_key, split_value))
        return context.transpose(1, 0, 2).reshape(-1, head_count * HD).astype(jnp.bfloat16)
    context_all = lax.map(cross, (memory, decoder, span_segment))
    context = context_all.reshape(N_DP, MB, N_TM, DTOK, CROSS_HEADS * HD).transpose(0, 2, 1, 3, 4)
    context = context.reshape(TOKALL, CROSS_HEADS * HD)
    out_grad = jnp.dot(context.T, cotangent, preferred_element_type=jnp.float32)
    return (context, out_grad)
```

```python
import functools

import jax
import jax.numpy as jnp
from jax import lax
from jax.experimental import pallas as pl
from jax.experimental.pallas import tpu as pltpu
from jax.sharding import PartitionSpec as P

HD = 64
BLK = 64
MB = 2

MESH = pl.DeviceIdType.MESH
epsilon = 1e-05
SCALE = HD ** (-0.5)


def norm_rows(inputs):
    values32 = inputs.astype(jnp.float32)
    center = values32 - jnp.mean(values32, axis=-1, keepdims=True)
    spread = jnp.mean(center * center, axis=-1, keepdims=True)
    return (center * lax.rsqrt(spread + epsilon)).astype(jnp.bfloat16)


def dot_nt(a, b):
    return lax.dot_general(a, b, (((1,), (1,)), ((), ())), preferred_element_type=jnp.float32)


def dot_nn(a, b):
    return jnp.dot(a, b, preferred_element_type=jnp.float32)


def kernel(
    sizes,
    frames,
    enc_mask,
    cross_mask,
    dec,
    cot,
    qkv,
    out_w,
    query_w,
    both_w,
    context_out,
    grad_out,
    xbuf,
    ybuf,
    kvbuf,
    memn,
    qall,
    part,
    part_in,
    ctx_all,
    cot_all,
    x_send,
    x_recv,
    halo_send,
    halo_recv,
    mem_send,
    mem_recv,
    q_send,
    q_recv,
    part_send,
    part_recv,
    ctx_send,
    ctx_recv,
    cot_send,
    cot_recv,
):
    n_dp, n_sec, n_tm = sizes
    group = n_dp * n_tm
    dp, sec, tm = (lax.axis_index(a) for a in ("dp", "section", "tm"))
    me = dp * n_tm + tm
    rows = frames.shape[1]
    width = out_w.shape[0]
    heads = width // HD
    cross_width = query_w.shape[1]
    cross_heads = cross_width // HD
    chunks = rows // BLK
    tokens = qall.shape[2]
    first, last = sec == 0, sec == n_sec - 1

    def peer(d):
        other = lax.rem(me + d, group)
        return other, {"dp": other // n_tm, "tm": lax.rem(other, n_tm)}

    def remote(src, dst, send, recv, where):
        return pltpu.make_async_remote_copy(
            src_ref=src, dst_ref=dst, send_sem=send, recv_sem=recv, device_id=where, device_id_type=MESH
        )

    def each(count, body, start=0):
        lax.fori_loop(start, count, lambda i, c: (body(i), c)[1], 0)

    def x_copy(m):
        return remote(ybuf.at[m], xbuf.at[m], x_send.at[m], x_recv.at[m], {"section": sec + 1})

    def halo_up(m):
        return remote(
            kvbuf.at[m, pl.ds(rows, BLK)], kvbuf.at[m, pl.ds(0, BLK)],
            halo_send.at[0, m], halo_recv.at[0, m], {"tm": tm + 1},
        )

    def halo_down(m):
        return remote(
            kvbuf.at[m, pl.ds(BLK, BLK)], kvbuf.at[m, pl.ds(rows + BLK, BLK)],
            halo_send.at[1, m], halo_recv.at[1, m], {"tm": tm - 1},
        )

    def mem_copy(m, c):
        return remote(
            memn.at[m, pl.ds(c * BLK, BLK)], memn.at[m, pl.ds(c * BLK, BLK)],
            mem_send.at[m, c], mem_recv.at[m, c], {"section": sec - 1},
        )

    def q_copy(d, slot, sem):
        return remote(
            qall.at[tm], qall.at[slot], q_send.at[d], q_recv.at[sem], {"tm": lax.rem(tm + d, n_tm)}
        )

    def part_copy(m, d, slot):
        to = lax.rem(tm + d, n_tm)
        return remote(
            part.at[m, to], part_in.at[slot, m], part_send.at[m, d], part_recv.at[m, slot], {"tm": to}
        )

    def ctx_copy(d, slot):
        _, where = peer(d)
        return remote(ctx_all.at[me], ctx_all.at[slot], ctx_send.at[d], ctx_recv.at[slot], where)

    def cot_copy(d, slot):
        other, where = peer(d)
        return remote(cot.at[other], cot_all.at[slot], cot_send.at[d], cot_recv.at[slot], where)

    for m in range(MB):
        kvbuf[m, 0:BLK, :] = jnp.zeros((BLK, 2 * width), jnp.bfloat16)
        kvbuf[m, rows + BLK :, :] = jnp.zeros((BLK, 2 * width), jnp.bfloat16)

    barrier = pltpu.get_barrier_semaphore()

    def greet(d):
        _, where = peer(d)
        pl.semaphore_signal(barrier, inc=1, device_id=where, device_id_type=MESH)

    each(group, greet, 1)

    @pl.when(sec > 0)
    def _():
        pl.semaphore_signal(barrier, inc=1, device_id={"section": sec - 1}, device_id_type=MESH)

    @pl.when(sec < n_sec - 1)
    def _():
        pl.semaphore_signal(barrier, inc=1, device_id={"section": sec + 1}, device_id_type=MESH)

    near = jnp.where(sec > 0, 1, 0) + jnp.where(sec < n_sec - 1, 1, 0)
    pl.semaphore_wait(barrier, group - 1 + near)

    each(group, lambda d: cot_copy(d, me).start(), 1)
    cot_all[me] = cot[me]

    def queries():
        values = dot_nn(norm_rows(dec[...]), query_w[...]).astype(jnp.bfloat16)
        qall[tm] = values.reshape(MB, tokens, cross_width)
        each(n_tm, lambda d: q_copy(d, tm, tm).start(), 1)

    @pl.when(sec > 0)
    def _():
        queries()

    def encode(m):
        @pl.when(first)
        def _():
            xbuf[m] = frames[m]

        @pl.when(sec > 0)
        def _():
            x_copy(m).wait_recv()

        normed = norm_rows(xbuf[m])
        kvbuf[m, BLK : BLK + rows, :] = dot_nn(normed, qkv[:, width:]).astype(jnp.bfloat16)

        @pl.when(tm < n_tm - 1)
        def _():
            halo_up(m).start()

        @pl.when(tm > 0)
        def _():
            halo_down(m).start()

        query = dot_nn(normed, qkv[:, :width]).astype(jnp.bfloat16)

        @pl.when(tm > 0)
        def _():
            halo_up(m).wait_recv()

        @pl.when(tm < n_tm - 1)
        def _():
            halo_down(m).wait_recv()

        seen = enc_mask[m] > 0
        parts = []
        for h in range(heads):
            cols = slice(h * HD, (h + 1) * HD)
            scores = dot_nt(query[:, cols], kvbuf[m, :, cols]) * SCALE
            weights = jnp.where(seen, jnp.exp(scores), 0.0)
            totals = jnp.sum(weights, axis=-1, keepdims=True)
            value = kvbuf[m, :, width + h * HD : width + (h + 1) * HD]
            parts.append((dot_nn(weights.astype(jnp.bfloat16), value) / totals).astype(jnp.bfloat16))
        attended = jnp.concatenate(parts, axis=1)
        update = dot_nn(attended, out_w[...])
        finished = (xbuf[m].astype(jnp.float32) + update).astype(jnp.bfloat16)

        @pl.when(sec < n_sec - 1)
        def _():
            ybuf[m] = finished
            x_copy(m).start()

        @pl.when(last)
        def _():
            memn[m] = norm_rows(finished)
            if n_sec > 1:
                for c in range(chunks):
                    mem_copy(m, c).start()

    each(MB, encode)

    @pl.when(first)
    def _():
        queries()

    def q_arrives(d):
        source = lax.rem(tm + n_tm - d, n_tm)
        q_copy(d, source, source).wait_recv()

    each(n_tm, q_arrives, 1)

    def cross(m):
        for c in range(chunks):
            @pl.when(sec < n_sec - 1)
            def _():
                mem_copy(m, c).wait_recv()

            @pl.when((sec < n_sec - 1) & (sec > 0))
            def _():
                mem_copy(m, c).start()

        key_value = dot_nn(memn[m], both_w[...]).astype(jnp.bfloat16)
        query = qall[:, m].reshape(n_tm * tokens, cross_width)
        seen = cross_mask[m] > 0
        sums, denominators = [], []
        for h in range(cross_heads):
            cols = slice(h * HD, (h + 1) * HD)
            scores = dot_nt(query[:, cols], key_value[:, cols]) * SCALE
            weights = jnp.where(seen, jnp.exp(scores), 0.0)
            denominators.append(
                jnp.broadcast_to(jnp.sum(weights, axis=-1, keepdims=True), (n_tm * tokens, HD))
            )
            value = key_value[:, cross_width + h * HD : cross_width + (h + 1) * HD]
            sums.append(dot_nn(weights.astype(jnp.bfloat16), value))
        both = jnp.concatenate(sums + denominators, axis=1)
        part[m] = both.reshape(n_tm, tokens, 2 * cross_width)
        each(n_tm, lambda d: part_copy(m, d, tm).start(), 1)

    each(MB, cross)

    for m in range(MB):
        total = part[m, tm]
        for d in range(1, n_tm):
            source = lax.rem(tm + n_tm - d, n_tm)
            part_copy(m, d, source).wait_recv()
            total = total + part_in[source, m]
        context = (total[:, :cross_width] / total[:, cross_width:]).astype(jnp.bfloat16)
        ctx_all[me, m * tokens : (m + 1) * tokens, :] = context
        context_out[m * tokens : (m + 1) * tokens, :] = context

    each(group, lambda d: ctx_copy(d, me).start(), 1)

    def arrivals(d):
        source = lax.rem(me + group - d, group)
        cot_copy(d, source).wait_recv()
        ctx_copy(d, source).wait_recv()

    each(group, arrivals, 1)
    left = ctx_all[...].reshape(group * MB * tokens, cross_width)
    right = cot_all[...].reshape(group * MB * tokens, cot.shape[2])
    grad_out[...] = lax.dot_general(
        left, right, (((0,), (0,)), ((), ())), preferred_element_type=jnp.float32
    )

    for m in range(MB):
        @pl.when(sec < n_sec - 1)
        def _():
            x_copy(m).wait_send()

        @pl.when(tm < n_tm - 1)
        def _():
            halo_up(m).wait_send()

        @pl.when(tm > 0)
        def _():
            halo_down(m).wait_send()

        @pl.when(sec > 0)
        def _():
            for c in range(chunks):
                mem_copy(m, c).wait_send()

        each(n_tm, lambda d: part_copy(m, d, tm).wait_send(), 1)
    each(n_tm, lambda d: q_copy(d, tm, tm).wait_send(), 1)

    def group_sent(d):
        cot_copy(d, me).wait_send()
        ctx_copy(d, me).wait_send()

    each(group, group_sent, 1)


def per_device(
    sizes,
    frames,
    block_mask,
    span_segment,
    dec_states,
    enc_qkv,
    enc_out,
    cross_query,
    cross_key,
    cross_value,
    cotangent,
):
    n_dp, n_sec, n_tm = sizes
    group = n_dp * n_tm
    qkv_full = lax.all_gather(enc_qkv[0], ("dp", "tm"), axis=0, tiled=True)
    out_full = lax.all_gather(enc_out[0], ("dp", "tm"), axis=1, tiled=True)
    cross_local = jnp.concatenate([cross_query, cross_key, cross_value], axis=1)
    cross_full = lax.all_gather(cross_local, ("dp", "tm"), axis=0, tiled=True)
    cross_width = cross_query.shape[1]
    query_full, both_full = cross_full[:, :cross_width], cross_full[:, cross_width:]
    tm = lax.axis_index("tm")
    rows, dim = frames.shape[1], frames.shape[2]
    width = out_full.shape[0]
    blocks = rows // BLK
    tokens = dec_states.shape[0] // MB

    index = tm * blocks + jnp.arange(blocks, dtype=jnp.int32)
    left_open = (block_mask[:, :, 0] == 1) & (index > 0)
    right_open = (block_mask[:, :, 1] == 1) & (index < blocks * n_tm - 1)
    window = jnp.arange(rows + 2 * BLK, dtype=jnp.int32) // BLK - 1
    own = jnp.arange(blocks, dtype=jnp.int32)
    offset = window[None, None, :] - own[None, :, None]
    seen = (
        (offset == 0)
        | ((offset == -1) & left_open[:, :, None])
        | ((offset == 1) & right_open[:, :, None])
    )
    enc_mask = jnp.repeat(seen.astype(jnp.float32), BLK, axis=1)
    segments = lax.dynamic_slice_in_dim(span_segment, tm * blocks, blocks, axis=1)
    frame_segment = jnp.repeat(segments, BLK, axis=1)
    token_segment = jnp.arange(n_tm * tokens, dtype=jnp.int32) // tokens
    cross_mask = (token_segment[None, :, None] == frame_segment[:, None, :]).astype(jnp.float32)
    cot = cotangent.reshape(MB * tokens, group, dim // group).transpose(1, 0, 2)

    bf, f32 = jnp.bfloat16, jnp.float32
    dma = pltpu.SemaphoreType.DMA
    vmem = pl.BlockSpec(memory_space=pltpu.VMEM)
    return pl.pallas_call(
        functools.partial(kernel, sizes),
        out_shape=(
            jax.ShapeDtypeStruct((MB * tokens, cross_width), bf),
            jax.ShapeDtypeStruct((cross_width, dim // group), f32),
        ),
        in_specs=[vmem] * 9,
        out_specs=(vmem, vmem),
        scratch_shapes=[
            pltpu.VMEM((MB, rows, dim), bf),
            pltpu.VMEM((MB, rows, dim), bf),
            pltpu.VMEM((MB, rows + 2 * BLK, 2 * width), bf),
            pltpu.VMEM((MB, rows, dim), bf),
            pltpu.VMEM((n_tm, MB, tokens, cross_width), bf),
            pltpu.VMEM((MB, n_tm, tokens, 2 * cross_width), f32),
            pltpu.VMEM((n_tm, MB, tokens, 2 * cross_width), f32),
            pltpu.VMEM((group, MB * tokens, cross_width), bf),
            pltpu.VMEM((group, MB * tokens, dim // group), bf),
            dma((MB,)),
            dma((MB,)),
            dma((2, MB)),
            dma((2, MB)),
            dma((MB, blocks)),
            dma((MB, blocks)),
            dma((n_tm,)),
            dma((n_tm,)),
            dma((MB, n_tm)),
            dma((MB, n_tm)),
            dma((group,)),
            dma((group,)),
            dma((group,)),
            dma((group,)),
        ],
        compiler_params=pltpu.CompilerParams(
            collective_id=0, has_side_effects=True, vmem_limit_bytes=56 * 2**20
        ),
    )(frames, enc_mask, cross_mask, dec_states, cot, qkv_full, out_full, query_full, both_full)


def solution(mesh):
    sizes = tuple(mesh.shape[a] for a in ("dp", "section", "tm"))
    in_specs = (
        P("dp", "tm", None),
        P("dp", "tm", None),
        P("dp", None),
        P(("dp", "tm"), None),
        P("section", ("dp", "tm"), None),
        P("section", None, ("dp", "tm")),
        P(("dp", "tm"), "section"),
        P(("dp", "tm"), "section"),
        P(("dp", "tm"), "section"),
        P(("dp", "tm"), None),
    )
    out_specs = (P(("dp", "tm"), "section"), P("section", ("dp", "tm")))
    return jax.shard_map(
        functools.partial(per_device, sizes),
        mesh=mesh,
        in_specs=in_specs,
        out_specs=out_specs,
        check_vma=False,
    )
```

```python
import functools

import jax
import jax.numpy as jnp
from jax import lax
from jax.experimental import pallas as pl
from jax.experimental.pallas import tpu as pltpu
from jax.sharding import PartitionSpec as P

HD = 64
BLK = 64
MB = 2

MESH = pl.DeviceIdType.MESH
epsilon = 1e-05
SCALE = HD ** (-0.5)


def norm_rows(inputs):
    values32 = inputs.astype(jnp.float32)
    center = values32 - jnp.mean(values32, axis=-1, keepdims=True)
    spread = jnp.mean(center * center, axis=-1, keepdims=True)
    return (center * lax.rsqrt(spread + epsilon)).astype(jnp.bfloat16)


def dot_nt(a, b):
    return lax.dot_general(a, b, (((1,), (1,)), ((), ())), preferred_element_type=jnp.float32)


def dot_nn(a, b):
    return jnp.dot(a, b, preferred_element_type=jnp.float32)


def kernel(
    sizes,
    spread,
    frames,
    enc_mask,
    cross_mask,
    dec,
    cot,
    qkv_in,
    out_in,
    query_in,
    key_in,
    value_in,
    context_out,
    grad_out,
    qkv,
    out_t,
    cross_w,
    xbuf,
    ybuf,
    kvbuf,
    memn,
    qall,
    part,
    part_in,
    ctx_all,
    cot_all,
    x_send,
    x_recv,
    halo_send,
    halo_recv,
    mem_send,
    mem_recv,
    q_send,
    q_recv,
    part_send,
    part_recv,
    ctx_send,
    ctx_recv,
    cot_send,
    cot_recv,
    w_send,
    w_recv,
):
    n_dp, n_sec, n_tm = sizes
    group = n_dp * n_tm
    dp, sec, tm = (lax.axis_index(a) for a in ("dp", "section", "tm"))
    me = dp * n_tm + tm
    rows = frames.shape[1]
    width = out_t.shape[1]
    heads = width // HD
    cross_width = query_in.shape[1]
    cross_heads = cross_width // HD
    chunks = rows // BLK
    tokens = qall.shape[2]
    first, last = sec == 0, sec == n_sec - 1

    def peer(d):
        other = lax.rem(me + d, group)
        return other, {"dp": other // n_tm, "tm": lax.rem(other, n_tm)}

    def remote(src, dst, send, recv, where):
        return pltpu.make_async_remote_copy(
            src_ref=src, dst_ref=dst, send_sem=send, recv_sem=recv, device_id=where, device_id_type=MESH
        )

    def each(count, body, start=0):
        lax.fori_loop(start, count, lambda i, c: (body(i), c)[1], 0)

    def x_copy(m):
        return remote(ybuf.at[m], xbuf.at[m], x_send.at[m], x_recv.at[m], {"section": sec + 1})

    def halo_up(m):
        return remote(
            kvbuf.at[m, pl.ds(rows, BLK)], kvbuf.at[m, pl.ds(0, BLK)],
            halo_send.at[0, m], halo_recv.at[0, m], {"tm": tm + 1},
        )

    def halo_down(m):
        return remote(
            kvbuf.at[m, pl.ds(BLK, BLK)], kvbuf.at[m, pl.ds(rows + BLK, BLK)],
            halo_send.at[1, m], halo_recv.at[1, m], {"tm": tm - 1},
        )

    def mem_copy(m, c):
        return remote(
            memn.at[m, pl.ds(c * BLK, BLK)], memn.at[m, pl.ds(c * BLK, BLK)],
            mem_send.at[m, c], mem_recv.at[m, c], {"section": sec - 1},
        )

    def q_copy(d, slot, sem):
        return remote(
            qall.at[tm], qall.at[slot], q_send.at[d], q_recv.at[sem], {"tm": lax.rem(tm + d, n_tm)}
        )

    def part_copy(m, d, slot):
        to = lax.rem(tm + d, n_tm)
        return remote(
            part.at[m, to], part_in.at[slot, m], part_send.at[m, d], part_recv.at[m, slot], {"tm": to}
        )

    def ctx_copy(d, slot):
        _, where = peer(d)
        return remote(ctx_all.at[me], ctx_all.at[slot], ctx_send.at[d], ctx_recv.at[slot], where)

    def cot_copy(d, slot):
        other, where = peer(d)
        return remote(cot.at[other], cot_all.at[slot], cot_send.at[d], cot_recv.at[slot], where)

    weights_of = (qkv, out_t, cross_w)
    share = qkv_in.shape[0]
    half = share // 2
    to_x = {"dp": 1 - dp}
    to_y = {"tm": lax.rem(tm + 2, n_tm)}
    to_core = {"tm": tm + 1 - 2 * lax.rem(tm, 2)}
    from_x = (1 - dp) * n_tm + tm
    from_y = dp * n_tm + lax.rem(tm + 2, n_tm)
    from_both = (1 - dp) * n_tm + lax.rem(tm + 2, n_tm)
    routes = [(me, 0, to_x), (me, 1, to_x), (me, 0, to_y), (me, 1, to_y), (from_x, 0, to_y), (from_y, 1, to_x)]
    routes += [(o, h, to_core) for o in (me, from_x, from_y, from_both) for h in (0, 1)]

    def w_copy(g, i):
        owner, h, where = routes[i]
        piece = weights_of[g].at[pl.ds(pl.multiple_of(owner * share + h * half, 16), half)]
        return remote(piece, piece, w_send.at[g, i], w_recv.at[g, i], where)

    def w_own(g):
        for i in (0, 3, 1, 2, 6, 7):
            w_copy(g, i).start()

    def w_forward(g):
        for got, passed in ((0, (4, 8)), (3, (5, 11))):
            w_copy(g, got).wait_recv()
            for i in passed:
                w_copy(g, i).start()

    def w_rest(g):
        for got, passed in ((1, 9), (2, 10), (4, 12), (5, 13)):
            w_copy(g, got).wait_recv()
            w_copy(g, passed).start()
        for i in range(6, 14):
            w_copy(g, i).wait_recv()

    for m in range(MB):
        kvbuf[m, 0:BLK, :] = jnp.zeros((BLK, 2 * width), jnp.bfloat16)
        kvbuf[m, rows + BLK :, :] = jnp.zeros((BLK, 2 * width), jnp.bfloat16)

    barrier = pltpu.get_barrier_semaphore()

    def greet(d):
        _, where = peer(d)
        pl.semaphore_signal(barrier, inc=1, device_id=where, device_id_type=MESH)

    each(group, greet, 1)

    @pl.when(sec > 0)
    def _():
        pl.semaphore_signal(barrier, inc=1, device_id={"section": sec - 1}, device_id_type=MESH)

    @pl.when(sec < n_sec - 1)
    def _():
        pl.semaphore_signal(barrier, inc=1, device_id={"section": sec + 1}, device_id_type=MESH)

    near = jnp.where(sec > 0, 1, 0) + jnp.where(sec < n_sec - 1, 1, 0)
    pl.semaphore_wait(barrier, group - 1 + near)

    base = pl.multiple_of(me * share, 16) if spread else 0
    mine = pl.ds(base, share)
    qkv[mine] = qkv_in[...]
    if spread:
        w_own(0)
    out_t[mine] = out_in[...].T
    cross_w[mine] = jnp.concatenate([key_in[...], value_in[...], query_in[...]], axis=1)
    cot_all[me] = cot[me]
    if spread:
        w_forward(0)
        w_own(1)
        w_rest(0)
        w_forward(1)
        w_own(2)

        @pl.when(sec > 0)
        def _():
            w_rest(1)
            w_forward(2)
            w_rest(2)

    each(group, lambda d: cot_copy(d, me).start(), 1)

    def queries():
        values = dot_nn(norm_rows(dec[...]), cross_w[:, 2 * cross_width :]).astype(jnp.bfloat16)
        qall[tm] = values.reshape(MB, tokens, cross_width)
        each(n_tm, lambda d: q_copy(d, tm, tm).start(), 1)

    @pl.when(sec > 0)
    def _():
        queries()

    def encode(m):
        @pl.when(first)
        def _():
            xbuf[m] = frames[m]

        @pl.when(sec > 0)
        def _():
            x_copy(m).wait_recv()

        normed = norm_rows(xbuf[m])
        kvbuf[m, BLK : BLK + rows, :] = dot_nn(normed, qkv[:, width:]).astype(jnp.bfloat16)

        @pl.when(tm < n_tm - 1)
        def _():
            halo_up(m).start()

        @pl.when(tm > 0)
        def _():
            halo_down(m).start()

        query = dot_nn(normed, qkv[:, :width]).astype(jnp.bfloat16)

        @pl.when(tm > 0)
        def _():
            halo_up(m).wait_recv()

        @pl.when(tm < n_tm - 1)
        def _():
            halo_down(m).wait_recv()

        seen = enc_mask[m] > 0
        parts = []
        for h in range(heads):
            cols = slice(h * HD, (h + 1) * HD)
            scores = dot_nt(query[:, cols], kvbuf[m, :, cols]) * SCALE
            weights = jnp.where(seen, jnp.exp(scores), 0.0)
            totals = jnp.sum(weights, axis=-1, keepdims=True)
            value = kvbuf[m, :, width + h * HD : width + (h + 1) * HD]
            parts.append((dot_nn(weights.astype(jnp.bfloat16), value) / totals).astype(jnp.bfloat16))
        attended = jnp.concatenate(parts, axis=1)
        if spread:
            @pl.when(first & (m == 0))
            def _():
                w_rest(1)

        update = dot_nt(attended, out_t[...])
        finished = (xbuf[m].astype(jnp.float32) + update).astype(jnp.bfloat16)

        @pl.when(sec < n_sec - 1)
        def _():
            ybuf[m] = finished
            x_copy(m).start()

        @pl.when(last)
        def _():
            memn[m] = norm_rows(finished)
            if n_sec > 1:
                for c in range(chunks):
                    mem_copy(m, c).start()

    each(MB, encode)

    @pl.when(first)
    def _():
        if spread:
            w_forward(2)
            w_rest(2)
        queries()

    def q_arrives(d):
        source = lax.rem(tm + n_tm - d, n_tm)
        q_copy(d, source, source).wait_recv()

    each(n_tm, q_arrives, 1)

    def cross(m):
        for c in range(chunks):
            @pl.when(sec < n_sec - 1)
            def _():
                mem_copy(m, c).wait_recv()

            @pl.when((sec < n_sec - 1) & (sec > 0))
            def _():
                mem_copy(m, c).start()

        key_value = dot_nn(memn[m], cross_w[:, : 2 * cross_width]).astype(jnp.bfloat16)
        query = qall[:, m].reshape(n_tm * tokens, cross_width)
        seen = cross_mask[m] > 0
        sums, denominators = [], []
        for h in range(cross_heads):
            cols = slice(h * HD, (h + 1) * HD)
            scores = dot_nt(query[:, cols], key_value[:, cols]) * SCALE
            weights = jnp.where(seen, jnp.exp(scores), 0.0)
            denominators.append(
                jnp.broadcast_to(jnp.sum(weights, axis=-1, keepdims=True), (n_tm * tokens, HD))
            )
            value = key_value[:, cross_width + h * HD : cross_width + (h + 1) * HD]
            sums.append(dot_nn(weights.astype(jnp.bfloat16), value))
        both = jnp.concatenate(sums + denominators, axis=1)
        part[m] = both.reshape(n_tm, tokens, 2 * cross_width)
        each(n_tm, lambda d: part_copy(m, d, tm).start(), 1)

    each(MB, cross)

    for m in range(MB):
        total = part[m, tm]
        for d in range(1, n_tm):
            source = lax.rem(tm + n_tm - d, n_tm)
            part_copy(m, d, source).wait_recv()
            total = total + part_in[source, m]
        context = (total[:, :cross_width] / total[:, cross_width:]).astype(jnp.bfloat16)
        ctx_all[me, m * tokens : (m + 1) * tokens, :] = context
        context_out[m * tokens : (m + 1) * tokens, :] = context

    each(group, lambda d: ctx_copy(d, me).start(), 1)

    def arrivals(d):
        source = lax.rem(me + group - d, group)
        cot_copy(d, source).wait_recv()
        ctx_copy(d, source).wait_recv()

    each(group, arrivals, 1)
    left = ctx_all[...].reshape(group * MB * tokens, cross_width)
    right = cot_all[...].reshape(group * MB * tokens, cot.shape[2])
    grad_out[...] = lax.dot_general(
        left, right, (((0,), (0,)), ((), ())), preferred_element_type=jnp.float32
    )

    for m in range(MB):
        @pl.when(sec < n_sec - 1)
        def _():
            x_copy(m).wait_send()

        @pl.when(tm < n_tm - 1)
        def _():
            halo_up(m).wait_send()

        @pl.when(tm > 0)
        def _():
            halo_down(m).wait_send()

        @pl.when(sec > 0)
        def _():
            for c in range(chunks):
                mem_copy(m, c).wait_send()

        each(n_tm, lambda d: part_copy(m, d, tm).wait_send(), 1)
    each(n_tm, lambda d: q_copy(d, tm, tm).wait_send(), 1)

    if spread:
        for g in range(3):
            for i in range(14):
                w_copy(g, i).wait_send()

    def group_sent(d):
        cot_copy(d, me).wait_send()
        ctx_copy(d, me).wait_send()

    each(group, group_sent, 1)


def per_device(
    sizes,
    frames,
    block_mask,
    span_segment,
    dec_states,
    enc_qkv,
    enc_out,
    cross_query,
    cross_key,
    cross_value,
    cotangent,
):
    n_dp, n_sec, n_tm = sizes
    group = n_dp * n_tm
    qkv_w, out_w = enc_qkv[0], enc_out[0]
    spread = n_dp == 2 and n_tm == 4 and qkv_w.shape[0] % 32 == 0 and out_w.shape[1] == qkv_w.shape[0]
    if not spread:
        qkv_w = lax.all_gather(qkv_w, ("dp", "tm"), axis=0, tiled=True)
        out_w = lax.all_gather(out_w, ("dp", "tm"), axis=1, tiled=True)
        cross_query, cross_key, cross_value = (
            lax.all_gather(w, ("dp", "tm"), axis=0, tiled=True)
            for w in (cross_query, cross_key, cross_value)
        )
    cross_width = cross_query.shape[1]
    tm = lax.axis_index("tm")
    rows, dim = frames.shape[1], frames.shape[2]
    width = out_w.shape[0]
    blocks = rows // BLK
    tokens = dec_states.shape[0] // MB

    index = tm * blocks + jnp.arange(blocks, dtype=jnp.int32)
    left_open = (block_mask[:, :, 0] == 1) & (index > 0)
    right_open = (block_mask[:, :, 1] == 1) & (index < blocks * n_tm - 1)
    window = jnp.arange(rows + 2 * BLK, dtype=jnp.int32) // BLK - 1
    own = jnp.arange(blocks, dtype=jnp.int32)
    offset = window[None, None, :] - own[None, :, None]
    seen = (
        (offset == 0)
        | ((offset == -1) & left_open[:, :, None])
        | ((offset == 1) & right_open[:, :, None])
    )
    enc_mask = jnp.repeat(seen.astype(jnp.float32), BLK, axis=1)
    segments = lax.dynamic_slice_in_dim(span_segment, tm * blocks, blocks, axis=1)
    frame_segment = jnp.repeat(segments, BLK, axis=1)
    token_segment = jnp.arange(n_tm * tokens, dtype=jnp.int32) // tokens
    cross_mask = (token_segment[None, :, None] == frame_segment[:, None, :]).astype(jnp.float32)
    cot = cotangent.reshape(MB * tokens, group, dim // group).transpose(1, 0, 2)

    bf, f32 = jnp.bfloat16, jnp.float32
    dma = pltpu.SemaphoreType.DMA
    vmem = pl.BlockSpec(memory_space=pltpu.VMEM)
    return pl.pallas_call(
        functools.partial(kernel, sizes, spread),
        out_shape=(
            jax.ShapeDtypeStruct((MB * tokens, cross_width), bf),
            jax.ShapeDtypeStruct((cross_width, dim // group), f32),
        ),
        in_specs=[vmem] * 10,
        out_specs=(vmem, vmem),
        scratch_shapes=[
            pltpu.VMEM((dim, 3 * width), bf),
            pltpu.VMEM((dim, width), bf),
            pltpu.VMEM((dim, 3 * cross_width), bf),
            pltpu.VMEM((MB, rows, dim), bf),
            pltpu.VMEM((MB, rows, dim), bf),
            pltpu.VMEM((MB, rows + 2 * BLK, 2 * width), bf),
            pltpu.VMEM((MB, rows, dim), bf),
            pltpu.VMEM((n_tm, MB, tokens, cross_width), bf),
            pltpu.VMEM((MB, n_tm, tokens, 2 * cross_width), f32),
            pltpu.VMEM((n_tm, MB, tokens, 2 * cross_width), f32),
            pltpu.VMEM((group, MB * tokens, cross_width), bf),
            pltpu.VMEM((group, MB * tokens, dim // group), bf),
            dma((MB,)),
            dma((MB,)),
            dma((2, MB)),
            dma((2, MB)),
            dma((MB, blocks)),
            dma((MB, blocks)),
            dma((n_tm,)),
            dma((n_tm,)),
            dma((MB, n_tm)),
            dma((MB, n_tm)),
            dma((group,)),
            dma((group,)),
            dma((group,)),
            dma((group,)),
            dma((3, 14)),
            dma((3, 14)),
        ],
        compiler_params=pltpu.CompilerParams(
            collective_id=0, has_side_effects=True, vmem_limit_bytes=56 * 2**20
        ),
    )(frames, enc_mask, cross_mask, dec_states, cot, qkv_w, out_w, cross_query, cross_key, cross_value)


def solution(mesh):
    sizes = tuple(mesh.shape[a] for a in ("dp", "section", "tm"))
    in_specs = (
        P("dp", "tm", None),
        P("dp", "tm", None),
        P("dp", None),
        P(("dp", "tm"), None),
        P("section", ("dp", "tm"), None),
        P("section", None, ("dp", "tm")),
        P(("dp", "tm"), "section"),
        P(("dp", "tm"), "section"),
        P(("dp", "tm"), "section"),
        P(("dp", "tm"), None),
    )
    out_specs = (P(("dp", "tm"), "section"), P("section", ("dp", "tm")))
    return jax.shard_map(
        functools.partial(per_device, sizes),
        mesh=mesh,
        in_specs=in_specs,
        out_specs=out_specs,
        check_vma=False,
    )
```

```python
import functools

import jax
import jax.numpy as jnp
from jax import lax
from jax.experimental import pallas as pl
from jax.experimental.pallas import tpu as pltpu
from jax.sharding import PartitionSpec as P

HD = 64
BLK = 64
MB = 2
PIECE = 32

MESH = pl.DeviceIdType.MESH
epsilon = 1e-05
SCALE = HD ** (-0.5)


def norm_rows(inputs):
    values32 = inputs.astype(jnp.float32)
    center = values32 - jnp.mean(values32, axis=-1, keepdims=True)
    spread = jnp.mean(center * center, axis=-1, keepdims=True)
    return (center * lax.rsqrt(spread + epsilon)).astype(jnp.bfloat16)


def dot_nt(a, b):
    return lax.dot_general(a, b, (((1,), (1,)), ((), ())), preferred_element_type=jnp.float32)


def dot_nn(a, b):
    return jnp.dot(a, b, preferred_element_type=jnp.float32)


def kernel(
    sizes,
    spread,
    frames,
    block_mask,
    span,
    dec,
    cot,
    qkv_in,
    out_in,
    query_in,
    key_in,
    value_in,
    context_out,
    grad_out,
    qkv,
    out_t,
    cross_w,
    enc_mask,
    cross_mask,
    cot_split,
    xbuf,
    ybuf,
    kvbuf,
    memn,
    qall,
    part,
    part_in,
    ctx_all,
    cot_all,
    x_send,
    x_recv,
    halo_send,
    halo_recv,
    mem_send,
    mem_recv,
    q_send,
    q_recv,
    part_send,
    part_recv,
    ctx_send,
    ctx_recv,
    cot_send,
    cot_recv,
    w_send,
    w_recv,
):
    n_dp, n_sec, n_tm = sizes
    group = n_dp * n_tm
    dp, sec, tm = (lax.axis_index(a) for a in ("dp", "section", "tm"))
    me = dp * n_tm + tm
    rows = frames.shape[1]
    width = out_t.shape[1]
    heads = width // HD
    cross_width = query_in.shape[1]
    cross_heads = cross_width // HD
    chunks = rows // PIECE
    tokens = qall.shape[2]
    first, last = sec == 0, sec == n_sec - 1

    def peer(d):
        other = lax.rem(me + d, group)
        return other, {"dp": other // n_tm, "tm": lax.rem(other, n_tm)}

    def remote(src, dst, send, recv, where):
        return pltpu.make_async_remote_copy(
            src_ref=src, dst_ref=dst, send_sem=send, recv_sem=recv, device_id=where, device_id_type=MESH
        )

    def each(count, body, start=0):
        lax.fori_loop(start, count, lambda i, c: (body(i), c)[1], 0)

    def x_copy(m):
        return remote(ybuf.at[m], xbuf.at[m], x_send.at[m], x_recv.at[m], {"section": sec + 1})

    def halo_up(m):
        return remote(
            kvbuf.at[m, pl.ds(rows, BLK)], kvbuf.at[m, pl.ds(0, BLK)],
            halo_send.at[0, m], halo_recv.at[0, m], {"tm": tm + 1},
        )

    def halo_down(m):
        return remote(
            kvbuf.at[m, pl.ds(BLK, BLK)], kvbuf.at[m, pl.ds(rows + BLK, BLK)],
            halo_send.at[1, m], halo_recv.at[1, m], {"tm": tm - 1},
        )

    def mem_copy(m, c):
        return remote(
            memn.at[m, pl.ds(c * PIECE, PIECE)], memn.at[m, pl.ds(c * PIECE, PIECE)],
            mem_send.at[m, c], mem_recv.at[m, c], {"section": sec - 1},
        )

    def q_copy(d, slot, sem):
        return remote(
            qall.at[tm], qall.at[slot], q_send.at[d], q_recv.at[sem], {"tm": lax.rem(tm + d, n_tm)}
        )

    def part_copy(m, d, slot):
        to = lax.rem(tm + d, n_tm)
        return remote(
            part.at[m, to], part_in.at[slot, m], part_send.at[m, d], part_recv.at[m, slot], {"tm": to}
        )

    def ctx_copy(d, slot):
        _, where = peer(d)
        return remote(ctx_all.at[me], ctx_all.at[slot], ctx_send.at[d], ctx_recv.at[slot], where)

    def cot_copy(d, slot):
        other, where = peer(d)
        return remote(cot_split.at[other], cot_all.at[slot], cot_send.at[d], cot_recv.at[slot], where)

    weights_of = (qkv, out_t, cross_w)
    share = qkv_in.shape[0]
    half = share // 2
    to_x = {"dp": 1 - dp}
    to_y = {"tm": lax.rem(tm + 2, n_tm)}
    to_core = {"tm": tm + 1 - 2 * lax.rem(tm, 2)}
    from_x = (1 - dp) * n_tm + tm
    from_y = dp * n_tm + lax.rem(tm + 2, n_tm)
    from_both = (1 - dp) * n_tm + lax.rem(tm + 2, n_tm)
    routes = [(me, 0, to_x), (me, 1, to_x), (me, 0, to_y), (me, 1, to_y), (from_x, 0, to_y), (from_y, 1, to_x)]
    routes += [(o, h, to_core) for o in (me, from_x, from_y, from_both) for h in (0, 1)]

    def w_copy(g, i):
        owner, h, where = routes[i]
        piece = weights_of[g].at[pl.ds(pl.multiple_of(owner * share + h * half, 16), half)]
        return remote(piece, piece, w_send.at[g, i], w_recv.at[g, i], where)

    def w_own(g):
        for i in (0, 3, 1, 2, 6, 7):
            w_copy(g, i).start()

    def w_forward(g):
        for got, passed in ((0, (4, 8)), (3, (5, 11))):
            w_copy(g, got).wait_recv()
            for i in passed:
                w_copy(g, i).start()

    def w_rest(g):
        for got, passed in ((1, 9), (2, 10), (4, 12), (5, 13)):
            w_copy(g, got).wait_recv()
            w_copy(g, passed).start()
        for i in range(6, 14):
            w_copy(g, i).wait_recv()

    for m in range(MB):
        kvbuf[m, 0:BLK, :] = jnp.zeros((BLK, 2 * width), jnp.bfloat16)
        kvbuf[m, rows + BLK :, :] = jnp.zeros((BLK, 2 * width), jnp.bfloat16)

    barrier = pltpu.get_barrier_semaphore()

    def greet(d):
        _, where = peer(d)
        pl.semaphore_signal(barrier, inc=1, device_id=where, device_id_type=MESH)

    each(group, greet, 1)

    @pl.when(sec > 0)
    def _():
        pl.semaphore_signal(barrier, inc=1, device_id={"section": sec - 1}, device_id_type=MESH)

    @pl.when(sec < n_sec - 1)
    def _():
        pl.semaphore_signal(barrier, inc=1, device_id={"section": sec + 1}, device_id_type=MESH)

    near = jnp.where(sec > 0, 1, 0) + jnp.where(sec < n_sec - 1, 1, 0)
    pl.semaphore_wait(barrier, group - 1 + near)

    share_cols = cot_split.shape[2]

    def make_masks():
        blocks = rows // BLK
        column = lax.broadcasted_iota(jnp.int32, (BLK, rows + 2 * BLK), 1) // BLK
        frame_block = lax.broadcasted_iota(jnp.int32, (1, rows), 1) // BLK
        row_segment = lax.broadcasted_iota(jnp.int32, (n_tm * tokens, rows), 0) // tokens
        for m in range(MB):
            served = jnp.zeros((1, rows), jnp.int32)
            segments = span[m : m + 1, :]
            place = lax.broadcasted_iota(jnp.int32, segments.shape, 1)
            for b in range(blocks):
                index = tm * blocks + b
                before = jnp.where(index > 0, block_mask[m, b : b + 1, 0:1], 0)
                after = jnp.where(index < n_tm * blocks - 1, block_mask[m, b : b + 1, 1:2], 0)
                seen = jnp.where(column == b + 1, 1, 0)
                seen = jnp.where(column == b, before, seen)
                seen = jnp.where(column == b + 2, after, seen)
                enc_mask[m, b * BLK : (b + 1) * BLK, :] = seen.astype(jnp.float32)
                one = jnp.sum(
                    jnp.where(place == index, segments, 0).astype(jnp.float32), axis=1, keepdims=True
                ).astype(jnp.int32)
                served = jnp.where(frame_block == b, one, served)
            cross_mask[m] = jnp.where(row_segment == served, 1.0, 0.0)

    base = pl.multiple_of(me * share, 16) if spread else 0
    mine = pl.ds(base, share)
    qkv[mine] = qkv_in[...]
    if spread:
        w_own(0)
    out_t[mine] = out_in[...]
    cross_w[mine] = jnp.concatenate([key_in[...], value_in[...], query_in[...]], axis=1)
    for i in range(group):
        cot_split[i] = cot[:, i * share_cols : (i + 1) * share_cols]
    cot_all[me] = cot_split[me]
    make_masks()
    if spread:
        w_forward(0)
        w_own(1)
        w_rest(0)
        w_forward(1)
        w_own(2)

        @pl.when(sec > 0)
        def _():
            w_rest(1)
            w_forward(2)
            w_rest(2)

    each(group, lambda d: cot_copy(d, me).start(), 1)

    def queries():
        values = dot_nn(norm_rows(dec[...]), cross_w[:, 2 * cross_width :]).astype(jnp.bfloat16)
        qall[tm] = values.reshape(MB, tokens, cross_width)
        each(n_tm, lambda d: q_copy(d, tm, tm).start(), 1)

    @pl.when(sec > 0)
    def _():
        queries()

    def encode(m):
        @pl.when(first)
        def _():
            xbuf[m] = frames[m]

        @pl.when(sec > 0)
        def _():
            x_copy(m).wait_recv()

        normed = norm_rows(xbuf[m])
        kvbuf[m, BLK : BLK + rows, :] = dot_nn(normed, qkv[:, width:]).astype(jnp.bfloat16)

        @pl.when(tm < n_tm - 1)
        def _():
            halo_up(m).start()

        @pl.when(tm > 0)
        def _():
            halo_down(m).start()

        query = dot_nn(normed, qkv[:, :width]).astype(jnp.bfloat16)

        @pl.when(tm > 0)
        def _():
            halo_up(m).wait_recv()

        @pl.when(tm < n_tm - 1)
        def _():
            halo_down(m).wait_recv()

        seen = enc_mask[m] > 0
        parts = []
        for h in range(heads):
            cols = slice(h * HD, (h + 1) * HD)
            scores = dot_nt(query[:, cols], kvbuf[m, :, cols]) * SCALE
            weights = jnp.where(seen, jnp.exp(scores), 0.0)
            totals = jnp.sum(weights, axis=-1, keepdims=True)
            value = kvbuf[m, :, width + h * HD : width + (h + 1) * HD]
            parts.append((dot_nn(weights.astype(jnp.bfloat16), value) / totals).astype(jnp.bfloat16))
        attended = jnp.concatenate(parts, axis=1)
        if spread:
            @pl.when(first & (m == 0))
            def _():
                w_rest(1)

        update = dot_nt(attended, out_t[...])
        finished = (xbuf[m].astype(jnp.float32) + update).astype(jnp.bfloat16)

        @pl.when(sec < n_sec - 1)
        def _():
            ybuf[m] = finished
            x_copy(m).start()

        @pl.when(last)
        def _():
            memn[m] = norm_rows(finished)
            if n_sec > 1:
                for c in range(chunks):
                    mem_copy(m, c).start()

    each(MB, encode)

    @pl.when(first)
    def _():
        if spread:
            w_forward(2)
            w_rest(2)
        queries()

    def q_arrives(d):
        source = lax.rem(tm + n_tm - d, n_tm)
        q_copy(d, source, source).wait_recv()

    each(n_tm, q_arrives, 1)

    def cross(m):
        for c in range(chunks):
            @pl.when(sec < n_sec - 1)
            def _():
                mem_copy(m, c).wait_recv()

            @pl.when((sec < n_sec - 1) & (sec > 0))
            def _():
                mem_copy(m, c).start()

        key_value = dot_nn(memn[m], cross_w[:, : 2 * cross_width]).astype(jnp.bfloat16)
        query = qall[:, m].reshape(n_tm * tokens, cross_width)
        seen = cross_mask[m] > 0
        sums, denominators = [], []
        for h in range(cross_heads):
            cols = slice(h * HD, (h + 1) * HD)
            scores = dot_nt(query[:, cols], key_value[:, cols]) * SCALE
            weights = jnp.where(seen, jnp.exp(scores), 0.0)
            denominators.append(
                jnp.broadcast_to(jnp.sum(weights, axis=-1, keepdims=True), (n_tm * tokens, HD))
            )
            value = key_value[:, cross_width + h * HD : cross_width + (h + 1) * HD]
            sums.append(dot_nn(weights.astype(jnp.bfloat16), value))
        both = jnp.concatenate(sums + denominators, axis=1)
        part[m] = both.reshape(n_tm, tokens, 2 * cross_width)
        each(n_tm, lambda d: part_copy(m, d, tm).start(), 1)

    each(MB, cross)

    for m in range(MB):
        total = part[m, tm]
        for d in range(1, n_tm):
            source = lax.rem(tm + n_tm - d, n_tm)
            part_copy(m, d, source).wait_recv()
            total = total + part_in[source, m]
        context = (total[:, :cross_width] / total[:, cross_width:]).astype(jnp.bfloat16)
        ctx_all[me, m * tokens : (m + 1) * tokens, :] = context
        context_out[m * tokens : (m + 1) * tokens, :] = context

    each(group, lambda d: ctx_copy(d, me).start(), 1)

    def arrivals(d):
        source = lax.rem(me + group - d, group)
        cot_copy(d, source).wait_recv()
        ctx_copy(d, source).wait_recv()

    each(group, arrivals, 1)
    left = ctx_all[...].reshape(group * MB * tokens, cross_width)
    right = cot_all[...].reshape(group * MB * tokens, cot_split.shape[2])
    grad_out[...] = lax.dot_general(
        right, left, (((0,), (0,)), ((), ())), preferred_element_type=jnp.float32
    )

    for m in range(MB):
        @pl.when(sec < n_sec - 1)
        def _():
            x_copy(m).wait_send()

        @pl.when(tm < n_tm - 1)
        def _():
            halo_up(m).wait_send()

        @pl.when(tm > 0)
        def _():
            halo_down(m).wait_send()

        @pl.when(sec > 0)
        def _():
            for c in range(chunks):
                mem_copy(m, c).wait_send()

        each(n_tm, lambda d: part_copy(m, d, tm).wait_send(), 1)
    each(n_tm, lambda d: q_copy(d, tm, tm).wait_send(), 1)

    if spread:
        for g in range(3):
            for i in range(14):
                w_copy(g, i).wait_send()

    def group_sent(d):
        cot_copy(d, me).wait_send()
        ctx_copy(d, me).wait_send()

    each(group, group_sent, 1)


def per_device(
    sizes,
    frames,
    block_mask,
    span_segment,
    dec_states,
    enc_qkv,
    enc_out,
    cross_query,
    cross_key,
    cross_value,
    cotangent,
):
    n_dp, n_sec, n_tm = sizes
    group = n_dp * n_tm
    qkv_w, out_w = enc_qkv[0], enc_out[0].T
    spread = n_dp == 2 and n_tm == 4 and qkv_w.shape[0] % 32 == 0 and out_w.shape[0] == qkv_w.shape[0]
    if not spread:
        qkv_w = lax.all_gather(qkv_w, ("dp", "tm"), axis=0, tiled=True)
        out_w = lax.all_gather(out_w, ("dp", "tm"), axis=0, tiled=True)
        cross_query, cross_key, cross_value = (
            lax.all_gather(w, ("dp", "tm"), axis=0, tiled=True)
            for w in (cross_query, cross_key, cross_value)
        )
    cross_width = cross_query.shape[1]
    rows, dim = frames.shape[1], frames.shape[2]
    width = out_w.shape[1]
    tokens = dec_states.shape[0] // MB

    bf, f32 = jnp.bfloat16, jnp.float32
    dma = pltpu.SemaphoreType.DMA
    vmem = pl.BlockSpec(memory_space=pltpu.VMEM)
    context, grad_t = pl.pallas_call(
        functools.partial(kernel, sizes, spread),
        out_shape=(
            jax.ShapeDtypeStruct((MB * tokens, cross_width), bf),
            jax.ShapeDtypeStruct((dim // group, cross_width), f32),
        ),
        in_specs=[vmem] * 10,
        out_specs=(vmem, vmem),
        scratch_shapes=[
            pltpu.VMEM((dim, 3 * width), bf),
            pltpu.VMEM((dim, width), bf),
            pltpu.VMEM((dim, 3 * cross_width), bf),
            pltpu.VMEM((MB, rows, rows + 2 * BLK), f32),
            pltpu.VMEM((MB, n_tm * tokens, rows), f32),
            pltpu.VMEM((group, MB * tokens, dim // group), bf),
            pltpu.VMEM((MB, rows, dim), bf),
            pltpu.VMEM((MB, rows, dim), bf),
            pltpu.VMEM((MB, rows + 2 * BLK, 2 * width), bf),
            pltpu.VMEM((MB, rows, dim), bf),
            pltpu.VMEM((n_tm, MB, tokens, cross_width), bf),
            pltpu.VMEM((MB, n_tm, tokens, 2 * cross_width), f32),
            pltpu.VMEM((n_tm, MB, tokens, 2 * cross_width), f32),
            pltpu.VMEM((group, MB * tokens, cross_width), bf),
            pltpu.VMEM((group, MB * tokens, dim // group), bf),
            dma((MB,)),
            dma((MB,)),
            dma((2, MB)),
            dma((2, MB)),
            dma((MB, rows // PIECE)),
            dma((MB, rows // PIECE)),
            dma((n_tm,)),
            dma((n_tm,)),
            dma((MB, n_tm)),
            dma((MB, n_tm)),
            dma((group,)),
            dma((group,)),
            dma((group,)),
            dma((group,)),
            dma((3, 14)),
            dma((3, 14)),
        ],
        compiler_params=pltpu.CompilerParams(
            collective_id=0, has_side_effects=True, vmem_limit_bytes=56 * 2**20
        ),
    )(frames, block_mask, span_segment, dec_states, cotangent, qkv_w, out_w, cross_query, cross_key, cross_value)
    return context, grad_t.T


def solution(mesh):
    sizes = tuple(mesh.shape[a] for a in ("dp", "section", "tm"))
    in_specs = (
        P("dp", "tm", None),
        P("dp", "tm", None),
        P("dp", None),
        P(("dp", "tm"), None),
        P("section", ("dp", "tm"), None),
        P("section", None, ("dp", "tm")),
        P(("dp", "tm"), "section"),
        P(("dp", "tm"), "section"),
        P(("dp", "tm"), "section"),
        P(("dp", "tm"), None),
    )
    out_specs = (P(("dp", "tm"), "section"), P("section", ("dp", "tm")))
    return jax.shard_map(
        functools.partial(per_device, sizes),
        mesh=mesh,
        in_specs=in_specs,
        out_specs=out_specs,
        check_vma=False,
    )
```

```python
import functools

import jax
import jax.numpy as jnp
from jax import lax
from jax.experimental import pallas as pl
from jax.experimental.pallas import tpu as pltpu
from jax.sharding import PartitionSpec as P

HD = 64
BLK = 64
MB = 2
PIECE = 32

MESH = pl.DeviceIdType.MESH
epsilon = 1e-05
SCALE = HD ** (-0.5)


def norm_rows(inputs):
    values32 = inputs.astype(jnp.float32)
    center = values32 - jnp.mean(values32, axis=-1, keepdims=True)
    spread = jnp.mean(center * center, axis=-1, keepdims=True)
    return (center * lax.rsqrt(spread + epsilon)).astype(jnp.bfloat16)


def dot_nt(a, b):
    return lax.dot_general(a, b, (((1,), (1,)), ((), ())), preferred_element_type=jnp.float32)


def dot_nn(a, b):
    return jnp.dot(a, b, preferred_element_type=jnp.float32)


def kernel(
    sizes,
    spread,
    frames,
    block_mask,
    span,
    dec,
    cot,
    qkv_in,
    out_in,
    query_in,
    key_in,
    value_in,
    context_out,
    grad_out,
    qkv,
    out_t,
    cross_w,
    enc_mask,
    cross_mask,
    cot_split,
    xbuf,
    ybuf,
    kvbuf,
    memn,
    qall,
    part,
    part_in,
    ctx_all,
    cot_all,
    x_send,
    x_recv,
    halo_send,
    halo_recv,
    mem_send,
    mem_recv,
    q_send,
    q_recv,
    part_send,
    part_recv,
    ctx_send,
    ctx_recv,
    cot_send,
    cot_recv,
    w_send,
    w_recv,
):
    n_dp, n_sec, n_tm = sizes
    group = n_dp * n_tm
    dp, sec, tm = (lax.axis_index(a) for a in ("dp", "section", "tm"))
    me = dp * n_tm + tm
    rows = frames.shape[1]
    width = out_t.shape[1]
    heads = width // HD
    cross_width = query_in.shape[1]
    cross_heads = cross_width // HD
    chunks = rows // PIECE
    tokens = qall.shape[2]
    first, last = sec == 0, sec == n_sec - 1

    def peer(d):
        other = lax.rem(me + d, group)
        return other, {"dp": other // n_tm, "tm": lax.rem(other, n_tm)}

    def remote(src, dst, send, recv, where):
        return pltpu.make_async_remote_copy(
            src_ref=src, dst_ref=dst, send_sem=send, recv_sem=recv, device_id=where, device_id_type=MESH
        )

    def each(count, body, start=0):
        lax.fori_loop(start, count, lambda i, c: (body(i), c)[1], 0)

    def x_copy(m, b):
        block = pl.ds(b * BLK, BLK)
        return remote(
            ybuf.at[m, block], xbuf.at[m, block], x_send.at[m, b], x_recv.at[m, b], {"section": sec + 1}
        )

    def halo_up(m):
        return remote(
            kvbuf.at[m, pl.ds(rows, BLK)], kvbuf.at[m, pl.ds(0, BLK)],
            halo_send.at[0, m], halo_recv.at[0, m], {"tm": tm + 1},
        )

    def halo_down(m):
        return remote(
            kvbuf.at[m, pl.ds(BLK, BLK)], kvbuf.at[m, pl.ds(rows + BLK, BLK)],
            halo_send.at[1, m], halo_recv.at[1, m], {"tm": tm - 1},
        )

    def mem_copy(m, c):
        return remote(
            memn.at[m, pl.ds(c * PIECE, PIECE)], memn.at[m, pl.ds(c * PIECE, PIECE)],
            mem_send.at[m, c], mem_recv.at[m, c], {"section": sec - 1},
        )

    def q_copy(d, slot, sem):
        return remote(
            qall.at[tm], qall.at[slot], q_send.at[d], q_recv.at[sem], {"tm": lax.rem(tm + d, n_tm)}
        )

    def part_copy(m, d, slot):
        to = lax.rem(tm + d, n_tm)
        return remote(
            part.at[m, to], part_in.at[slot, m], part_send.at[m, d], part_recv.at[m, slot], {"tm": to}
        )

    def ctx_copy(d, slot):
        _, where = peer(d)
        return remote(ctx_all.at[me], ctx_all.at[slot], ctx_send.at[d], ctx_recv.at[slot], where)

    def cot_copy(d, slot):
        other, where = peer(d)
        return remote(cot_split.at[other], cot_all.at[slot], cot_send.at[d], cot_recv.at[slot], where)

    weights_of = (qkv, out_t, cross_w)
    share = qkv_in.shape[0]
    half = share // 2
    to_x = {"dp": 1 - dp}
    to_y = {"tm": lax.rem(tm + 2, n_tm)}
    to_core = {"tm": tm + 1 - 2 * lax.rem(tm, 2)}
    from_x = (1 - dp) * n_tm + tm
    from_y = dp * n_tm + lax.rem(tm + 2, n_tm)
    from_both = (1 - dp) * n_tm + lax.rem(tm + 2, n_tm)
    routes = [(me, 0, to_x), (me, 1, to_x), (me, 0, to_y), (me, 1, to_y), (from_x, 0, to_y), (from_y, 1, to_x)]
    routes += [(o, h, to_core) for o in (me, from_x, from_y, from_both) for h in (0, 1)]

    def w_copy(g, i):
        owner, h, where = routes[i]
        piece = weights_of[g].at[pl.ds(pl.multiple_of(owner * share + h * half, 16), half)]
        return remote(piece, piece, w_send.at[g, i], w_recv.at[g, i], where)

    def w_own(g):
        for i in (0, 3, 1, 2, 6, 7):
            w_copy(g, i).start()

    def w_forward(g):
        for got, passed in ((0, (4, 8)), (3, (5, 11))):
            w_copy(g, got).wait_recv()
            for i in passed:
                w_copy(g, i).start()

    def w_rest(g):
        for got, passed in ((1, 9), (2, 10), (4, 12), (5, 13)):
            w_copy(g, got).wait_recv()
            w_copy(g, passed).start()
        for i in range(6, 14):
            w_copy(g, i).wait_recv()

    for m in range(MB):
        kvbuf[m, 0:BLK, :] = jnp.zeros((BLK, 2 * width), jnp.bfloat16)
        kvbuf[m, rows + BLK :, :] = jnp.zeros((BLK, 2 * width), jnp.bfloat16)

    barrier = pltpu.get_barrier_semaphore()

    def greet(d):
        _, where = peer(d)
        pl.semaphore_signal(barrier, inc=1, device_id=where, device_id_type=MESH)

    each(group, greet, 1)

    @pl.when(sec > 0)
    def _():
        pl.semaphore_signal(barrier, inc=1, device_id={"section": sec - 1}, device_id_type=MESH)

    @pl.when(sec < n_sec - 1)
    def _():
        pl.semaphore_signal(barrier, inc=1, device_id={"section": sec + 1}, device_id_type=MESH)

    near = jnp.where(sec > 0, 1, 0) + jnp.where(sec < n_sec - 1, 1, 0)
    pl.semaphore_wait(barrier, group - 1 + near)

    share_cols = cot_split.shape[2]

    def make_masks():
        blocks = rows // BLK
        column = lax.broadcasted_iota(jnp.int32, (BLK, 3 * BLK), 1) // BLK
        frame_block = lax.broadcasted_iota(jnp.int32, (1, rows), 1) // BLK
        row_segment = lax.broadcasted_iota(jnp.int32, (n_tm * tokens, rows), 0) // tokens
        for m in range(MB):
            served = jnp.zeros((1, rows), jnp.int32)
            segments = span[m : m + 1, :]
            place = lax.broadcasted_iota(jnp.int32, segments.shape, 1)
            for b in range(blocks):
                index = tm * blocks + b
                before = jnp.where(index > 0, block_mask[m, b : b + 1, 0:1], 0)
                after = jnp.where(index < n_tm * blocks - 1, block_mask[m, b : b + 1, 1:2], 0)
                seen = jnp.where(column == 0, before, jnp.where(column == 2, after, 1))
                enc_mask[m, b * BLK : (b + 1) * BLK, :] = seen.astype(jnp.float32)
                one = jnp.sum(
                    jnp.where(place == index, segments, 0).astype(jnp.float32), axis=1, keepdims=True
                ).astype(jnp.int32)
                served = jnp.where(frame_block == b, one, served)
            cross_mask[m] = jnp.where(row_segment == served, 1.0, 0.0)

    base = pl.multiple_of(me * share, 16) if spread else 0
    mine = pl.ds(base, share)
    qkv[mine] = qkv_in[...]
    if spread:
        w_own(0)
    out_t[mine] = out_in[...]
    cross_w[mine] = jnp.concatenate([key_in[...], value_in[...], query_in[...]], axis=1)
    for i in range(group):
        cot_split[i] = cot[:, i * share_cols : (i + 1) * share_cols]
    cot_all[me] = cot_split[me]
    make_masks()
    if spread:
        w_forward(0)
        w_own(1)
        w_rest(0)
        w_forward(1)
        w_own(2)

        @pl.when(sec > 0)
        def _():
            w_rest(1)
            w_forward(2)
            w_rest(2)

    each(group, lambda d: cot_copy(d, me).start(), 1)

    def queries():
        values = dot_nn(norm_rows(dec[...]), cross_w[:, 2 * cross_width :]).astype(jnp.bfloat16)
        qall[tm] = values.reshape(MB, tokens, cross_width)
        each(n_tm, lambda d: q_copy(d, tm, tm).start(), 1)

    @pl.when(sec > 0)
    def _():
        queries()

    def encode(m):
        @pl.when(first)
        def _():
            xbuf[m] = frames[m]

        pieces = []
        for b in range(rows // BLK):
            @pl.when(sec > 0)
            def _():
                x_copy(m, b).wait_recv()

            pieces.append(norm_rows(xbuf[m, b * BLK : (b + 1) * BLK, :]))
        normed = jnp.concatenate(pieces, axis=0)
        kvbuf[m, BLK : BLK + rows, :] = dot_nn(normed, qkv[:, width:]).astype(jnp.bfloat16)

        @pl.when(tm < n_tm - 1)
        def _():
            halo_up(m).start()

        @pl.when(tm > 0)
        def _():
            halo_down(m).start()

        query = dot_nn(normed, qkv[:, :width]).astype(jnp.bfloat16)

        for b in range(rows // BLK):
            if b == 0:
                @pl.when(tm > 0)
                def _():
                    halo_up(m).wait_recv()

            if b == rows // BLK - 1:
                @pl.when(tm < n_tm - 1)
                def _():
                    halo_down(m).wait_recv()

            block = slice(b * BLK, (b + 1) * BLK)
            around = slice(b * BLK, (b + 3) * BLK)
            seen = enc_mask[m, block, :] > 0
            parts = []
            for h in range(heads):
                cols = slice(h * HD, (h + 1) * HD)
                scores = dot_nt(query[block, cols], kvbuf[m, around, cols]) * SCALE
                weights = jnp.where(seen, jnp.exp(scores), 0.0)
                totals = jnp.sum(weights, axis=-1, keepdims=True)
                value = kvbuf[m, around, width + h * HD : width + (h + 1) * HD]
                parts.append((dot_nn(weights.astype(jnp.bfloat16), value) / totals).astype(jnp.bfloat16))
            attended = jnp.concatenate(parts, axis=1)
            if spread and b == 0:
                @pl.when(first & (m == 0))
                def _():
                    w_rest(1)

            update = dot_nt(attended, out_t[...])
            finished = (xbuf[m, block, :].astype(jnp.float32) + update).astype(jnp.bfloat16)

            @pl.when(sec < n_sec - 1)
            def _():
                ybuf[m, block, :] = finished
                x_copy(m, b).start()

            @pl.when(last)
            def _():
                memn[m, block, :] = norm_rows(finished)
                if n_sec > 1:
                    for c in range(b * BLK // PIECE, (b + 1) * BLK // PIECE):
                        mem_copy(m, c).start()

    each(MB, encode)

    @pl.when(first)
    def _():
        if spread:
            w_forward(2)
            w_rest(2)
        queries()

    def q_arrives(d):
        source = lax.rem(tm + n_tm - d, n_tm)
        q_copy(d, source, source).wait_recv()

    each(n_tm, q_arrives, 1)

    def cross(m):
        for c in range(chunks):
            @pl.when(sec < n_sec - 1)
            def _():
                mem_copy(m, c).wait_recv()

            @pl.when((sec < n_sec - 1) & (sec > 0))
            def _():
                mem_copy(m, c).start()

        key_value = dot_nn(memn[m], cross_w[:, : 2 * cross_width]).astype(jnp.bfloat16)
        query = qall[:, m].reshape(n_tm * tokens, cross_width)
        seen = cross_mask[m] > 0
        sums, denominators = [], []
        for h in range(cross_heads):
            cols = slice(h * HD, (h + 1) * HD)
            scores = dot_nt(query[:, cols], key_value[:, cols]) * SCALE
            weights = jnp.where(seen, jnp.exp(scores), 0.0)
            denominators.append(
                jnp.broadcast_to(jnp.sum(weights, axis=-1, keepdims=True), (n_tm * tokens, HD))
            )
            value = key_value[:, cross_width + h * HD : cross_width + (h + 1) * HD]
            sums.append(dot_nn(weights.astype(jnp.bfloat16), value))
        both = jnp.concatenate(sums + denominators, axis=1)
        part[m] = both.reshape(n_tm, tokens, 2 * cross_width)
        each(n_tm, lambda d: part_copy(m, d, tm).start(), 1)

    each(MB, cross)

    for m in range(MB):
        total = part[m, tm]
        for d in range(1, n_tm):
            source = lax.rem(tm + n_tm - d, n_tm)
            part_copy(m, d, source).wait_recv()
            total = total + part_in[source, m]
        context = (total[:, :cross_width] / total[:, cross_width:]).astype(jnp.bfloat16)
        ctx_all[me, m * tokens : (m + 1) * tokens, :] = context
        context_out[m * tokens : (m + 1) * tokens, :] = context

    each(group, lambda d: ctx_copy(d, me).start(), 1)

    def arrivals(d):
        source = lax.rem(me + group - d, group)
        cot_copy(d, source).wait_recv()
        ctx_copy(d, source).wait_recv()

    each(group, arrivals, 1)
    left = ctx_all[...].reshape(group * MB * tokens, cross_width)
    right = cot_all[...].reshape(group * MB * tokens, cot_split.shape[2])
    grad_out[...] = lax.dot_general(
        right, left, (((0,), (0,)), ((), ())), preferred_element_type=jnp.float32
    )

    for m in range(MB):
        @pl.when(sec < n_sec - 1)
        def _():
            for b in range(rows // BLK):
                x_copy(m, b).wait_send()

        @pl.when(tm < n_tm - 1)
        def _():
            halo_up(m).wait_send()

        @pl.when(tm > 0)
        def _():
            halo_down(m).wait_send()

        @pl.when(sec > 0)
        def _():
            for c in range(chunks):
                mem_copy(m, c).wait_send()

        each(n_tm, lambda d: part_copy(m, d, tm).wait_send(), 1)
    each(n_tm, lambda d: q_copy(d, tm, tm).wait_send(), 1)

    if spread:
        for g in range(3):
            for i in range(14):
                w_copy(g, i).wait_send()

    def group_sent(d):
        cot_copy(d, me).wait_send()
        ctx_copy(d, me).wait_send()

    each(group, group_sent, 1)


def per_device(
    sizes,
    frames,
    block_mask,
    span_segment,
    dec_states,
    enc_qkv,
    enc_out,
    cross_query,
    cross_key,
    cross_value,
    cotangent,
):
    n_dp, n_sec, n_tm = sizes
    group = n_dp * n_tm
    qkv_w, out_w = enc_qkv[0], enc_out[0].T
    spread = n_dp == 2 and n_tm == 4 and qkv_w.shape[0] % 32 == 0 and out_w.shape[0] == qkv_w.shape[0]
    if not spread:
        qkv_w = lax.all_gather(qkv_w, ("dp", "tm"), axis=0, tiled=True)
        out_w = lax.all_gather(out_w, ("dp", "tm"), axis=0, tiled=True)
        cross_query, cross_key, cross_value = (
            lax.all_gather(w, ("dp", "tm"), axis=0, tiled=True)
            for w in (cross_query, cross_key, cross_value)
        )
    cross_width = cross_query.shape[1]
    rows, dim = frames.shape[1], frames.shape[2]
    width = out_w.shape[1]
    tokens = dec_states.shape[0] // MB

    bf, f32 = jnp.bfloat16, jnp.float32
    dma = pltpu.SemaphoreType.DMA
    vmem = pl.BlockSpec(memory_space=pltpu.VMEM)
    context, grad_t = pl.pallas_call(
        functools.partial(kernel, sizes, spread),
        out_shape=(
            jax.ShapeDtypeStruct((MB * tokens, cross_width), bf),
            jax.ShapeDtypeStruct((dim // group, cross_width), f32),
        ),
        in_specs=[vmem] * 10,
        out_specs=(vmem, vmem),
        scratch_shapes=[
            pltpu.VMEM((dim, 3 * width), bf),
            pltpu.VMEM((dim, width), bf),
            pltpu.VMEM((dim, 3 * cross_width), bf),
            pltpu.VMEM((MB, rows, 3 * BLK), f32),
            pltpu.VMEM((MB, n_tm * tokens, rows), f32),
            pltpu.VMEM((group, MB * tokens, dim // group), bf),
            pltpu.VMEM((MB, rows, dim), bf),
            pltpu.VMEM((MB, rows, dim), bf),
            pltpu.VMEM((MB, rows + 2 * BLK, 2 * width), bf),
            pltpu.VMEM((MB, rows, dim), bf),
            pltpu.VMEM((n_tm, MB, tokens, cross_width), bf),
            pltpu.VMEM((MB, n_tm, tokens, 2 * cross_width), f32),
            pltpu.VMEM((n_tm, MB, tokens, 2 * cross_width), f32),
            pltpu.VMEM((group, MB * tokens, cross_width), bf),
            pltpu.VMEM((group, MB * tokens, dim // group), bf),
            dma((MB, rows // BLK)),
            dma((MB, rows // BLK)),
            dma((2, MB)),
            dma((2, MB)),
            dma((MB, rows // PIECE)),
            dma((MB, rows // PIECE)),
            dma((n_tm,)),
            dma((n_tm,)),
            dma((MB, n_tm)),
            dma((MB, n_tm)),
            dma((group,)),
            dma((group,)),
            dma((group,)),
            dma((group,)),
            dma((3, 14)),
            dma((3, 14)),
        ],
        compiler_params=pltpu.CompilerParams(
            collective_id=0, has_side_effects=True, vmem_limit_bytes=56 * 2**20
        ),
    )(frames, block_mask, span_segment, dec_states, cotangent, qkv_w, out_w, cross_query, cross_key, cross_value)
    return context, grad_t.T


def solution(mesh):
    sizes = tuple(mesh.shape[a] for a in ("dp", "section", "tm"))
    in_specs = (
        P("dp", "tm", None),
        P("dp", "tm", None),
        P("dp", None),
        P(("dp", "tm"), None),
        P("section", ("dp", "tm"), None),
        P("section", None, ("dp", "tm")),
        P(("dp", "tm"), "section"),
        P(("dp", "tm"), "section"),
        P(("dp", "tm"), "section"),
        P(("dp", "tm"), None),
    )
    out_specs = (P(("dp", "tm"), "section"), P("section", ("dp", "tm")))
    return jax.shard_map(
        functools.partial(per_device, sizes),
        mesh=mesh,
        in_specs=in_specs,
        out_specs=out_specs,
        check_vma=False,
    )
```

```python
import functools

import jax
import jax.numpy as jnp
from jax import lax
from jax.experimental import pallas as pl
from jax.experimental.pallas import tpu as pltpu
from jax.sharding import PartitionSpec as P

HD = 64
BLK = 64
MB = 2
PIECE = 32

MESH = pl.DeviceIdType.MESH
epsilon = 1e-05
SCALE = HD ** (-0.5)


def norm_rows(inputs):
    values32 = inputs.astype(jnp.float32)
    center = values32 - jnp.mean(values32, axis=-1, keepdims=True)
    spread = jnp.mean(center * center, axis=-1, keepdims=True)
    return (center * lax.rsqrt(spread + epsilon)).astype(jnp.bfloat16)


def dot_nt(a, b):
    return lax.dot_general(a, b, (((1,), (1,)), ((), ())), preferred_element_type=jnp.float32)


def dot_nn(a, b):
    return jnp.dot(a, b, preferred_element_type=jnp.float32)


def kernel(
    sizes,
    spread,
    frames,
    block_mask,
    span,
    dec,
    cot,
    qkv_in,
    out_in,
    query_in,
    key_in,
    value_in,
    context_out,
    grad_out,
    qkv,
    out_t,
    cross_w,
    enc_mask,
    cross_mask,
    cot_split,
    xbuf,
    ybuf,
    kvbuf,
    memn,
    qall,
    part,
    part_in,
    ctx_all,
    cot_all,
    x_send,
    x_recv,
    halo_send,
    halo_recv,
    mem_send,
    mem_recv,
    q_send,
    q_recv,
    part_send,
    part_recv,
    ctx_send,
    ctx_recv,
    cot_send,
    cot_recv,
    w_send,
    w_recv,
):
    n_dp, n_sec, n_tm = sizes
    group = n_dp * n_tm
    dp, sec, tm = (lax.axis_index(a) for a in ("dp", "section", "tm"))
    me = dp * n_tm + tm
    rows = frames.shape[1]
    width = out_t.shape[1]
    heads = width // HD
    cross_width = query_in.shape[1]
    cross_heads = cross_width // HD
    chunks = rows // PIECE
    tokens = qall.shape[2]
    first, last = sec == 0, sec == n_sec - 1

    def peer(d):
        other = lax.rem(me + d, group)
        return other, {"dp": other // n_tm, "tm": lax.rem(other, n_tm)}

    def remote(src, dst, send, recv, where):
        return pltpu.make_async_remote_copy(
            src_ref=src, dst_ref=dst, send_sem=send, recv_sem=recv, device_id=where, device_id_type=MESH
        )

    def each(count, body, start=0):
        lax.fori_loop(start, count, lambda i, c: (body(i), c)[1], 0)

    def x_copy(m):
        return remote(ybuf.at[m], xbuf.at[m], x_send.at[m], x_recv.at[m], {"section": sec + 1})

    def halo_up(m):
        return remote(
            kvbuf.at[m, pl.ds(rows, BLK)], kvbuf.at[m, pl.ds(0, BLK)],
            halo_send.at[0, m], halo_recv.at[0, m], {"tm": tm + 1},
        )

    def halo_down(m):
        return remote(
            kvbuf.at[m, pl.ds(BLK, BLK)], kvbuf.at[m, pl.ds(rows + BLK, BLK)],
            halo_send.at[1, m], halo_recv.at[1, m], {"tm": tm - 1},
        )

    def mem_copy(m, c):
        return remote(
            memn.at[m, pl.ds(c * PIECE, PIECE)], memn.at[m, pl.ds(c * PIECE, PIECE)],
            mem_send.at[m, c], mem_recv.at[m, c], {"section": sec - 1},
        )

    def q_copy(d, slot, sem):
        return remote(
            qall.at[tm], qall.at[slot], q_send.at[d], q_recv.at[sem], {"tm": lax.rem(tm + d, n_tm)}
        )

    def part_copy(m, d, slot):
        to = lax.rem(tm + d, n_tm)
        return remote(
            part.at[m, to], part_in.at[slot, m], part_send.at[m, d], part_recv.at[m, slot], {"tm": to}
        )

    def ctx_copy(d, slot):
        _, where = peer(d)
        return remote(ctx_all.at[me], ctx_all.at[slot], ctx_send.at[d], ctx_recv.at[slot], where)

    def cot_copy(d, slot):
        other, where = peer(d)
        return remote(cot_split.at[other], cot_all.at[slot], cot_send.at[d], cot_recv.at[slot], where)

    weights_of = (qkv, out_t, cross_w)
    share = qkv_in.shape[0]
    half = share // 2
    to_x = {"dp": 1 - dp}
    to_y = {"tm": lax.rem(tm + 2, n_tm)}
    to_core = {"tm": tm + 1 - 2 * lax.rem(tm, 2)}
    from_x = (1 - dp) * n_tm + tm
    from_y = dp * n_tm + lax.rem(tm + 2, n_tm)
    from_both = (1 - dp) * n_tm + lax.rem(tm + 2, n_tm)
    routes = [(me, 0, to_x), (me, 1, to_x), (me, 0, to_y), (me, 1, to_y), (from_x, 0, to_y), (from_y, 1, to_x)]
    routes += [(o, h, to_core) for o in (me, from_x, from_y, from_both) for h in (0, 1)]

    def w_copy(g, i):
        owner, h, where = routes[i]
        piece = weights_of[g].at[pl.ds(pl.multiple_of(owner * share + h * half, 16), half)]
        return remote(piece, piece, w_send.at[g, i], w_recv.at[g, i], where)

    def w_own(g):
        for i in (0, 3, 1, 2, 6, 7):
            w_copy(g, i).start()

    def w_forward(g):
        for got, passed in ((0, (4, 8)), (3, (5, 11))):
            w_copy(g, got).wait_recv()
            for i in passed:
                w_copy(g, i).start()

    def w_rest(g):
        for got, passed in ((1, 9), (2, 10), (4, 12), (5, 13)):
            w_copy(g, got).wait_recv()
            w_copy(g, passed).start()
        for i in range(6, 14):
            w_copy(g, i).wait_recv()

    for m in range(MB):
        kvbuf[m, 0:BLK, :] = jnp.zeros((BLK, 2 * width), jnp.bfloat16)
        kvbuf[m, rows + BLK :, :] = jnp.zeros((BLK, 2 * width), jnp.bfloat16)

    barrier = pltpu.get_barrier_semaphore()

    def greet(d):
        _, where = peer(d)
        pl.semaphore_signal(barrier, inc=1, device_id=where, device_id_type=MESH)

    each(group, greet, 1)

    @pl.when(sec > 0)
    def _():
        pl.semaphore_signal(barrier, inc=1, device_id={"section": sec - 1}, device_id_type=MESH)

    @pl.when(sec < n_sec - 1)
    def _():
        pl.semaphore_signal(barrier, inc=1, device_id={"section": sec + 1}, device_id_type=MESH)

    near = jnp.where(sec > 0, 1, 0) + jnp.where(sec < n_sec - 1, 1, 0)
    pl.semaphore_wait(barrier, group - 1 + near)

    share_cols = cot_split.shape[2]

    def make_masks():
        blocks = rows // BLK
        column = lax.broadcasted_iota(jnp.int32, (BLK, rows + 2 * BLK), 1) // BLK
        frame_block = lax.broadcasted_iota(jnp.int32, (1, rows), 1) // BLK
        row_segment = lax.broadcasted_iota(jnp.int32, (n_tm * tokens, rows), 0) // tokens
        for m in range(MB):
            served = jnp.zeros((1, rows), jnp.int32)
            segments = span[m : m + 1, :]
            place = lax.broadcasted_iota(jnp.int32, segments.shape, 1)
            for b in range(blocks):
                index = tm * blocks + b
                before = jnp.where(index > 0, block_mask[m, b : b + 1, 0:1], 0)
                after = jnp.where(index < n_tm * blocks - 1, block_mask[m, b : b + 1, 1:2], 0)
                seen = jnp.where(column == b + 1, 1, 0)
                seen = jnp.where(column == b, before, seen)
                seen = jnp.where(column == b + 2, after, seen)
                enc_mask[m, b * BLK : (b + 1) * BLK, :] = seen.astype(jnp.float32)
                one = jnp.sum(
                    jnp.where(place == index, segments, 0).astype(jnp.float32), axis=1, keepdims=True
                ).astype(jnp.int32)
                served = jnp.where(frame_block == b, one, served)
            cross_mask[m] = jnp.where(row_segment == served, 1.0, 0.0)

    base = pl.multiple_of(me * share, 16) if spread else 0
    mine = pl.ds(base, share)
    qkv[mine] = qkv_in[...]
    if spread:
        w_own(0)
    out_t[mine] = out_in[...]
    cross_w[mine] = jnp.concatenate([key_in[...], value_in[...], query_in[...]], axis=1)
    for i in range(group):
        cot_split[i] = cot[:, i * share_cols : (i + 1) * share_cols]
    cot_all[me] = cot_split[me]
    make_masks()
    if spread:
        w_forward(0)
        w_own(1)
        w_rest(0)
        w_forward(1)
        w_own(2)

        @pl.when(sec > 0)
        def _():
            w_rest(1)
            w_forward(2)
            w_rest(2)

    each(group, lambda d: cot_copy(d, me).start(), 1)

    def queries():
        values = dot_nn(norm_rows(dec[...]), cross_w[:, 2 * cross_width :]).astype(jnp.bfloat16)
        qall[tm] = values.reshape(MB, tokens, cross_width)
        each(n_tm, lambda d: q_copy(d, tm, tm).start(), 1)

    @pl.when(sec > 0)
    def _():
        queries()

    def encode(m):
        @pl.when(first)
        def _():
            xbuf[m] = frames[m]

        @pl.when(sec > 0)
        def _():
            x_copy(m).wait_recv()

        normed = norm_rows(xbuf[m])
        kvbuf[m, BLK : BLK + rows, :] = dot_nn(normed, qkv[:, width:]).astype(jnp.bfloat16)

        @pl.when(tm < n_tm - 1)
        def _():
            halo_up(m).start()

        @pl.when(tm > 0)
        def _():
            halo_down(m).start()

        query = dot_nn(normed, qkv[:, :width]) * SCALE
        low = lax.broadcasted_iota(jnp.int32, (rows, 2 * HD), 1) < HD

        @pl.when(tm > 0)
        def _():
            halo_up(m).wait_recv()

        @pl.when(tm < n_tm - 1)
        def _():
            halo_down(m).wait_recv()

        seen = jnp.concatenate([enc_mask[m], enc_mask[m]], axis=0) > 0
        parts = []
        for pair in range(heads // 2):
            cols = slice(pair * 2 * HD, (pair + 1) * 2 * HD)
            mixed = query[:, cols]
            stacked = jnp.concatenate(
                [jnp.where(low, mixed, 0.0), jnp.where(low, 0.0, mixed)], axis=0
            ).astype(jnp.bfloat16)
            weights = jnp.where(seen, jnp.exp(dot_nt(stacked, kvbuf[m, :, cols])), 0.0)
            totals = jnp.sum(weights, axis=-1, keepdims=True)
            value = kvbuf[m, :, width + pair * 2 * HD : width + (pair + 1) * 2 * HD]
            summed = dot_nn(weights.astype(jnp.bfloat16), value)
            top = jnp.where(low, summed[:rows], summed[rows:])
            parts.append((top / jnp.where(low, totals[:rows], totals[rows:])).astype(jnp.bfloat16))
        attended = jnp.concatenate(parts, axis=1)
        if spread:
            @pl.when(first & (m == 0))
            def _():
                w_rest(1)

        update = dot_nt(attended, out_t[...])
        finished = (xbuf[m].astype(jnp.float32) + update).astype(jnp.bfloat16)

        @pl.when(sec < n_sec - 1)
        def _():
            ybuf[m] = finished
            x_copy(m).start()

        @pl.when(last)
        def _():
            memn[m] = norm_rows(finished)
            if n_sec > 1:
                for c in range(chunks):
                    mem_copy(m, c).start()

    each(MB, encode)

    @pl.when(first)
    def _():
        if spread:
            w_forward(2)
            w_rest(2)
        queries()

    def q_arrives(d):
        source = lax.rem(tm + n_tm - d, n_tm)
        q_copy(d, source, source).wait_recv()

    each(n_tm, q_arrives, 1)

    def cross(m):
        for c in range(chunks):
            @pl.when(sec < n_sec - 1)
            def _():
                mem_copy(m, c).wait_recv()

            @pl.when((sec < n_sec - 1) & (sec > 0))
            def _():
                mem_copy(m, c).start()

        key_value = dot_nn(memn[m], cross_w[:, : 2 * cross_width]).astype(jnp.bfloat16)
        query = qall[:, m].reshape(n_tm * tokens, cross_width)
        seen = cross_mask[m] > 0
        sums, denominators = [], []
        for h in range(cross_heads):
            cols = slice(h * HD, (h + 1) * HD)
            scores = dot_nt(query[:, cols], key_value[:, cols]) * SCALE
            weights = jnp.where(seen, jnp.exp(scores), 0.0)
            denominators.append(
                jnp.broadcast_to(jnp.sum(weights, axis=-1, keepdims=True), (n_tm * tokens, HD))
            )
            value = key_value[:, cross_width + h * HD : cross_width + (h + 1) * HD]
            sums.append(dot_nn(weights.astype(jnp.bfloat16), value))
        both = jnp.concatenate(sums + denominators, axis=1)
        part[m] = both.reshape(n_tm, tokens, 2 * cross_width)
        each(n_tm, lambda d: part_copy(m, d, tm).start(), 1)

    each(MB, cross)

    for m in range(MB):
        total = part[m, tm]
        for d in range(1, n_tm):
            source = lax.rem(tm + n_tm - d, n_tm)
            part_copy(m, d, source).wait_recv()
            total = total + part_in[source, m]
        context = (total[:, :cross_width] / total[:, cross_width:]).astype(jnp.bfloat16)
        ctx_all[me, m * tokens : (m + 1) * tokens, :] = context
        context_out[m * tokens : (m + 1) * tokens, :] = context

    each(group, lambda d: ctx_copy(d, me).start(), 1)

    def arrivals(d):
        source = lax.rem(me + group - d, group)
        cot_copy(d, source).wait_recv()
        ctx_copy(d, source).wait_recv()

    each(group, arrivals, 1)
    left = ctx_all[...].reshape(group * MB * tokens, cross_width)
    right = cot_all[...].reshape(group * MB * tokens, cot_split.shape[2])
    grad_out[...] = lax.dot_general(
        right, left, (((0,), (0,)), ((), ())), preferred_element_type=jnp.float32
    )

    for m in range(MB):
        @pl.when(sec < n_sec - 1)
        def _():
            x_copy(m).wait_send()

        @pl.when(tm < n_tm - 1)
        def _():
            halo_up(m).wait_send()

        @pl.when(tm > 0)
        def _():
            halo_down(m).wait_send()

        @pl.when(sec > 0)
        def _():
            for c in range(chunks):
                mem_copy(m, c).wait_send()

        each(n_tm, lambda d: part_copy(m, d, tm).wait_send(), 1)
    each(n_tm, lambda d: q_copy(d, tm, tm).wait_send(), 1)

    if spread:
        for g in range(3):
            for i in range(14):
                w_copy(g, i).wait_send()

    def group_sent(d):
        cot_copy(d, me).wait_send()
        ctx_copy(d, me).wait_send()

    each(group, group_sent, 1)


def per_device(
    sizes,
    frames,
    block_mask,
    span_segment,
    dec_states,
    enc_qkv,
    enc_out,
    cross_query,
    cross_key,
    cross_value,
    cotangent,
):
    n_dp, n_sec, n_tm = sizes
    group = n_dp * n_tm
    qkv_w, out_w = enc_qkv[0], enc_out[0].T
    spread = n_dp == 2 and n_tm == 4 and qkv_w.shape[0] % 32 == 0 and out_w.shape[0] == qkv_w.shape[0]
    if not spread:
        qkv_w = lax.all_gather(qkv_w, ("dp", "tm"), axis=0, tiled=True)
        out_w = lax.all_gather(out_w, ("dp", "tm"), axis=0, tiled=True)
        cross_query, cross_key, cross_value = (
            lax.all_gather(w, ("dp", "tm"), axis=0, tiled=True)
            for w in (cross_query, cross_key, cross_value)
        )
    cross_width = cross_query.shape[1]
    rows, dim = frames.shape[1], frames.shape[2]
    width = out_w.shape[1]
    tokens = dec_states.shape[0] // MB

    bf, f32 = jnp.bfloat16, jnp.float32
    dma = pltpu.SemaphoreType.DMA
    vmem = pl.BlockSpec(memory_space=pltpu.VMEM)
    context, grad_t = pl.pallas_call(
        functools.partial(kernel, sizes, spread),
        out_shape=(
            jax.ShapeDtypeStruct((MB * tokens, cross_width), bf),
            jax.ShapeDtypeStruct((dim // group, cross_width), f32),
        ),
        in_specs=[vmem] * 10,
        out_specs=(vmem, vmem),
        scratch_shapes=[
            pltpu.VMEM((dim, 3 * width), bf),
            pltpu.VMEM((dim, width), bf),
            pltpu.VMEM((dim, 3 * cross_width), bf),
            pltpu.VMEM((MB, rows, rows + 2 * BLK), f32),
            pltpu.VMEM((MB, n_tm * tokens, rows), f32),
            pltpu.VMEM((group, MB * tokens, dim // group), bf),
            pltpu.VMEM((MB, rows, dim), bf),
            pltpu.VMEM((MB, rows, dim), bf),
            pltpu.VMEM((MB, rows + 2 * BLK, 2 * width), bf),
            pltpu.VMEM((MB, rows, dim), bf),
            pltpu.VMEM((n_tm, MB, tokens, cross_width), bf),
            pltpu.VMEM((MB, n_tm, tokens, 2 * cross_width), f32),
            pltpu.VMEM((n_tm, MB, tokens, 2 * cross_width), f32),
            pltpu.VMEM((group, MB * tokens, cross_width), bf),
            pltpu.VMEM((group, MB * tokens, dim // group), bf),
            dma((MB,)),
            dma((MB,)),
            dma((2, MB)),
            dma((2, MB)),
            dma((MB, rows // PIECE)),
            dma((MB, rows // PIECE)),
            dma((n_tm,)),
            dma((n_tm,)),
            dma((MB, n_tm)),
            dma((MB, n_tm)),
            dma((group,)),
            dma((group,)),
            dma((group,)),
            dma((group,)),
            dma((3, 14)),
            dma((3, 14)),
        ],
        compiler_params=pltpu.CompilerParams(
            collective_id=0, has_side_effects=True, vmem_limit_bytes=56 * 2**20
        ),
    )(frames, block_mask, span_segment, dec_states, cotangent, qkv_w, out_w, cross_query, cross_key, cross_value)
    return context, grad_t.T


def solution(mesh):
    sizes = tuple(mesh.shape[a] for a in ("dp", "section", "tm"))
    in_specs = (
        P("dp", "tm", None),
        P("dp", "tm", None),
        P("dp", None),
        P(("dp", "tm"), None),
        P("section", ("dp", "tm"), None),
        P("section", None, ("dp", "tm")),
        P(("dp", "tm"), "section"),
        P(("dp", "tm"), "section"),
        P(("dp", "tm"), "section"),
        P(("dp", "tm"), None),
    )
    out_specs = (P(("dp", "tm"), "section"), P("section", ("dp", "tm")))
    return jax.shard_map(
        functools.partial(per_device, sizes),
        mesh=mesh,
        in_specs=in_specs,
        out_specs=out_specs,
        check_vma=False,
    )
```

```python
import functools

import jax
import jax.numpy as jnp
from jax import lax
from jax.experimental import pallas as pl
from jax.experimental.pallas import tpu as pltpu
from jax.sharding import PartitionSpec as P

HD = 64
BLK = 64
MB = 2
PIECE = 32

MESH = pl.DeviceIdType.MESH
epsilon = 1e-05
SCALE = HD ** (-0.5)


def norm_rows(inputs):
    values32 = inputs.astype(jnp.float32)
    center = values32 - jnp.mean(values32, axis=-1, keepdims=True)
    spread = jnp.mean(center * center, axis=-1, keepdims=True)
    return (center * lax.rsqrt(spread + epsilon)).astype(jnp.bfloat16)


def dot_nt(a, b):
    return lax.dot_general(a, b, (((1,), (1,)), ((), ())), preferred_element_type=jnp.float32)


def dot_nn(a, b):
    return jnp.dot(a, b, preferred_element_type=jnp.float32)


def kernel(
    sizes,
    spread,
    frames,
    block_mask,
    span,
    dec,
    cot,
    qkv_in,
    out_in,
    query_in,
    key_in,
    value_in,
    context_out,
    grad_out,
    qkv,
    out_t,
    cross_w,
    enc_mask,
    cross_mask,
    cot_split,
    xbuf,
    ybuf,
    kvbuf,
    memn,
    qall,
    part,
    part_in,
    ctx_all,
    cot_all,
    x_send,
    x_recv,
    halo_send,
    halo_recv,
    mem_send,
    mem_recv,
    q_send,
    q_recv,
    part_send,
    part_recv,
    ctx_send,
    ctx_recv,
    cot_send,
    cot_recv,
    w_send,
    w_recv,
):
    n_dp, n_sec, n_tm = sizes
    group = n_dp * n_tm
    dp, sec, tm = (lax.axis_index(a) for a in ("dp", "section", "tm"))
    me = dp * n_tm + tm
    rows = frames.shape[1]
    width = out_t.shape[1]
    heads = width // HD
    cross_width = query_in.shape[1]
    cross_heads = cross_width // HD
    chunks = rows // PIECE
    tokens = qall.shape[2]
    first, last = sec == 0, sec == n_sec - 1

    def peer(d):
        other = lax.rem(me + d, group)
        return other, {"dp": other // n_tm, "tm": lax.rem(other, n_tm)}

    def remote(src, dst, send, recv, where):
        return pltpu.make_async_remote_copy(
            src_ref=src, dst_ref=dst, send_sem=send, recv_sem=recv, device_id=where, device_id_type=MESH
        )

    def each(count, body, start=0):
        lax.fori_loop(start, count, lambda i, c: (body(i), c)[1], 0)

    def x_copy(m):
        return remote(ybuf.at[m], xbuf.at[m], x_send.at[m], x_recv.at[m], {"section": sec + 1})

    def halo_up(m):
        return remote(
            kvbuf.at[m, pl.ds(rows, BLK)], kvbuf.at[m, pl.ds(0, BLK)],
            halo_send.at[0, m], halo_recv.at[0, m], {"tm": tm + 1},
        )

    def halo_down(m):
        return remote(
            kvbuf.at[m, pl.ds(BLK, BLK)], kvbuf.at[m, pl.ds(rows + BLK, BLK)],
            halo_send.at[1, m], halo_recv.at[1, m], {"tm": tm - 1},
        )

    def mem_copy(m, c):
        return remote(
            memn.at[m, pl.ds(c * PIECE, PIECE)], memn.at[m, pl.ds(c * PIECE, PIECE)],
            mem_send.at[m, c], mem_recv.at[m, c], {"section": sec - 1},
        )

    def q_copy(d, slot, sem):
        return remote(
            qall.at[tm], qall.at[slot], q_send.at[d], q_recv.at[sem], {"tm": lax.rem(tm + d, n_tm)}
        )

    def part_copy(m, d, slot):
        to = lax.rem(tm + d, n_tm)
        return remote(
            part.at[m, to], part_in.at[slot, m], part_send.at[m, d], part_recv.at[m, slot], {"tm": to}
        )

    def ctx_copy(d, slot):
        _, where = peer(d)
        return remote(ctx_all.at[me], ctx_all.at[slot], ctx_send.at[d], ctx_recv.at[slot], where)

    def cot_copy(d, slot):
        other, where = peer(d)
        return remote(cot_split.at[other], cot_all.at[slot], cot_send.at[d], cot_recv.at[slot], where)

    weights_of = (qkv, out_t, cross_w)
    share = qkv_in.shape[0]
    half = share // 2
    to_x = {"dp": 1 - dp}
    to_y = {"tm": lax.rem(tm + 2, n_tm)}
    to_core = {"tm": tm + 1 - 2 * lax.rem(tm, 2)}
    from_x = (1 - dp) * n_tm + tm
    from_y = dp * n_tm + lax.rem(tm + 2, n_tm)
    from_both = (1 - dp) * n_tm + lax.rem(tm + 2, n_tm)
    routes = [(me, 0, to_x), (me, 1, to_x), (me, 0, to_y), (me, 1, to_y), (from_x, 0, to_y), (from_y, 1, to_x)]
    routes += [(o, h, to_core) for o in (me, from_x, from_y, from_both) for h in (0, 1)]

    def w_copy(g, i):
        owner, h, where = routes[i]
        piece = weights_of[g].at[pl.ds(pl.multiple_of(owner * share + h * half, 16), half)]
        return remote(piece, piece, w_send.at[g, i], w_recv.at[g, i], where)

    def w_own(g):
        for i in (0, 3, 1, 2, 6, 7):
            w_copy(g, i).start()

    def w_forward(g):
        for got, passed in ((0, (4, 8)), (3, (5, 11))):
            w_copy(g, got).wait_recv()
            for i in passed:
                w_copy(g, i).start()

    def cot_sends():
        each(group, lambda d: cot_copy(d, me).start(), 1)

    def w_rest(g):
        for got, passed in ((1, 9), (2, 10), (4, 12), (5, 13)):
            w_copy(g, got).wait_recv()
            w_copy(g, passed).start()
        for i in range(6, 14):
            w_copy(g, i).wait_recv()

    for m in range(MB):
        kvbuf[m, 0:BLK, :] = jnp.zeros((BLK, 2 * width), jnp.bfloat16)
        kvbuf[m, rows + BLK :, :] = jnp.zeros((BLK, 2 * width), jnp.bfloat16)

    barrier = pltpu.get_barrier_semaphore()

    def greet(d):
        _, where = peer(d)
        pl.semaphore_signal(barrier, inc=1, device_id=where, device_id_type=MESH)

    each(group, greet, 1)

    @pl.when(sec > 0)
    def _():
        pl.semaphore_signal(barrier, inc=1, device_id={"section": sec - 1}, device_id_type=MESH)

    @pl.when(sec < n_sec - 1)
    def _():
        pl.semaphore_signal(barrier, inc=1, device_id={"section": sec + 1}, device_id_type=MESH)

    near = jnp.where(sec > 0, 1, 0) + jnp.where(sec < n_sec - 1, 1, 0)
    pl.semaphore_wait(barrier, group - 1 + near)

    share_cols = cot_split.shape[2]

    def make_masks():
        blocks = rows // BLK
        column = lax.broadcasted_iota(jnp.int32, (BLK, rows + 2 * BLK), 1) // BLK
        frame_block = lax.broadcasted_iota(jnp.int32, (1, rows), 1) // BLK
        row_segment = lax.broadcasted_iota(jnp.int32, (n_tm * tokens, rows), 0) // tokens
        for m in range(MB):
            served = jnp.zeros((1, rows), jnp.int32)
            segments = span[m : m + 1, :]
            place = lax.broadcasted_iota(jnp.int32, segments.shape, 1)
            for b in range(blocks):
                index = tm * blocks + b
                before = jnp.where(index > 0, block_mask[m, b : b + 1, 0:1], 0)
                after = jnp.where(index < n_tm * blocks - 1, block_mask[m, b : b + 1, 1:2], 0)
                seen = jnp.where(column == b + 1, 1, 0)
                seen = jnp.where(column == b, before, seen)
                seen = jnp.where(column == b + 2, after, seen)
                enc_mask[m, b * BLK : (b + 1) * BLK, :] = seen.astype(jnp.float32)
                one = jnp.sum(
                    jnp.where(place == index, segments, 0).astype(jnp.float32), axis=1, keepdims=True
                ).astype(jnp.int32)
                served = jnp.where(frame_block == b, one, served)
            cross_mask[m] = jnp.where(row_segment == served, 1.0, 0.0)

    base = pl.multiple_of(me * share, 16) if spread else 0
    mine = pl.ds(base, share)
    qkv[mine] = qkv_in[...]
    if spread:
        w_own(0)
    out_t[mine] = out_in[...]
    cross_w[mine] = jnp.concatenate([key_in[...], value_in[...], query_in[...]], axis=1)
    for i in range(group):
        cot_split[i] = cot[:, i * share_cols : (i + 1) * share_cols]
    cot_all[me] = cot_split[me]
    make_masks()
    if spread:
        w_forward(0)
        w_own(1)
        w_rest(0)
        w_forward(1)

        @pl.when(sec > 0)
        def _():
            w_own(2)
            cot_sends()
            w_rest(1)
            w_forward(2)
            w_rest(2)

    if not spread:
        cot_sends()

    def queries():
        values = dot_nn(norm_rows(dec[...]), cross_w[:, 2 * cross_width :]).astype(jnp.bfloat16)
        qall[tm] = values.reshape(MB, tokens, cross_width)
        each(n_tm, lambda d: q_copy(d, tm, tm).start(), 1)

    @pl.when(sec > 0)
    def _():
        queries()

    def encode(m):
        @pl.when(first)
        def _():
            xbuf[m] = frames[m]

        @pl.when(sec > 0)
        def _():
            x_copy(m).wait_recv()

        normed = norm_rows(xbuf[m])
        kvbuf[m, BLK : BLK + rows, :] = dot_nn(normed, qkv[:, width:]).astype(jnp.bfloat16)

        @pl.when(tm < n_tm - 1)
        def _():
            halo_up(m).start()

        @pl.when(tm > 0)
        def _():
            halo_down(m).start()

        query = dot_nn(normed, qkv[:, :width]).astype(jnp.bfloat16)

        @pl.when(tm > 0)
        def _():
            halo_up(m).wait_recv()

        @pl.when(tm < n_tm - 1)
        def _():
            halo_down(m).wait_recv()

        seen = enc_mask[m] > 0
        parts = []
        for h in range(heads):
            cols = slice(h * HD, (h + 1) * HD)
            scores = dot_nt(query[:, cols], kvbuf[m, :, cols]) * SCALE
            weights = jnp.where(seen, jnp.exp(scores), 0.0)
            totals = jnp.sum(weights, axis=-1, keepdims=True)
            value = kvbuf[m, :, width + h * HD : width + (h + 1) * HD]
            parts.append((dot_nn(weights.astype(jnp.bfloat16), value) / totals).astype(jnp.bfloat16))
        attended = jnp.concatenate(parts, axis=1)
        if spread:
            @pl.when(first & (m == 0))
            def _():
                w_rest(1)
                w_own(2)
                cot_sends()

        update = dot_nt(attended, out_t[...])
        finished = (xbuf[m].astype(jnp.float32) + update).astype(jnp.bfloat16)

        @pl.when(sec < n_sec - 1)
        def _():
            ybuf[m] = finished
            x_copy(m).start()

        @pl.when(last)
        def _():
            memn[m] = norm_rows(finished)
            if n_sec > 1:
                for c in range(chunks):
                    mem_copy(m, c).start()

    each(MB, encode)

    @pl.when(first)
    def _():
        if spread:
            w_forward(2)
            w_rest(2)
        queries()

    def q_arrives(d):
        source = lax.rem(tm + n_tm - d, n_tm)
        q_copy(d, source, source).wait_recv()

    each(n_tm, q_arrives, 1)

    def cross(m):
        for c in range(chunks):
            @pl.when(sec < n_sec - 1)
            def _():
                mem_copy(m, c).wait_recv()

            @pl.when((sec < n_sec - 1) & (sec > 0))
            def _():
                mem_copy(m, c).start()

        key_value = dot_nn(memn[m], cross_w[:, : 2 * cross_width]).astype(jnp.bfloat16)
        query = qall[:, m].reshape(n_tm * tokens, cross_width)
        seen = cross_mask[m] > 0
        sums, denominators = [], []
        for h in range(cross_heads):
            cols = slice(h * HD, (h + 1) * HD)
            scores = dot_nt(query[:, cols], key_value[:, cols]) * SCALE
            weights = jnp.where(seen, jnp.exp(scores), 0.0)
            denominators.append(
                jnp.broadcast_to(jnp.sum(weights, axis=-1, keepdims=True), (n_tm * tokens, HD))
            )
            value = key_value[:, cross_width + h * HD : cross_width + (h + 1) * HD]
            sums.append(dot_nn(weights.astype(jnp.bfloat16), value))
        both = jnp.concatenate(sums + denominators, axis=1)
        part[m] = both.reshape(n_tm, tokens, 2 * cross_width)
        each(n_tm, lambda d: part_copy(m, d, tm).start(), 1)

    each(MB, cross)

    for m in range(MB):
        total = part[m, tm]
        for d in range(1, n_tm):
            source = lax.rem(tm + n_tm - d, n_tm)
            part_copy(m, d, source).wait_recv()
            total = total + part_in[source, m]
        context = (total[:, :cross_width] / total[:, cross_width:]).astype(jnp.bfloat16)
        ctx_all[me, m * tokens : (m + 1) * tokens, :] = context
        context_out[m * tokens : (m + 1) * tokens, :] = context

    each(group, lambda d: ctx_copy(d, me).start(), 1)

    def arrivals(d):
        source = lax.rem(me + group - d, group)
        cot_copy(d, source).wait_recv()
        ctx_copy(d, source).wait_recv()

    each(group, arrivals, 1)
    left = ctx_all[...].reshape(group * MB * tokens, cross_width)
    right = cot_all[...].reshape(group * MB * tokens, cot_split.shape[2])
    grad_out[...] = lax.dot_general(
        right, left, (((0,), (0,)), ((), ())), preferred_element_type=jnp.float32
    )

    for m in range(MB):
        @pl.when(sec < n_sec - 1)
        def _():
            x_copy(m).wait_send()

        @pl.when(tm < n_tm - 1)
        def _():
            halo_up(m).wait_send()

        @pl.when(tm > 0)
        def _():
            halo_down(m).wait_send()

        @pl.when(sec > 0)
        def _():
            for c in range(chunks):
                mem_copy(m, c).wait_send()

        each(n_tm, lambda d: part_copy(m, d, tm).wait_send(), 1)
    each(n_tm, lambda d: q_copy(d, tm, tm).wait_send(), 1)

    if spread:
        for g in range(3):
            for i in range(14):
                w_copy(g, i).wait_send()

    def group_sent(d):
        cot_copy(d, me).wait_send()
        ctx_copy(d, me).wait_send()

    each(group, group_sent, 1)


def per_device(
    sizes,
    frames,
    block_mask,
    span_segment,
    dec_states,
    enc_qkv,
    enc_out,
    cross_query,
    cross_key,
    cross_value,
    cotangent,
):
    n_dp, n_sec, n_tm = sizes
    group = n_dp * n_tm
    qkv_w, out_w = enc_qkv[0], enc_out[0].T
    spread = n_dp == 2 and n_tm == 4 and qkv_w.shape[0] % 32 == 0 and out_w.shape[0] == qkv_w.shape[0]
    if not spread:
        qkv_w = lax.all_gather(qkv_w, ("dp", "tm"), axis=0, tiled=True)
        out_w = lax.all_gather(out_w, ("dp", "tm"), axis=0, tiled=True)
        cross_query, cross_key, cross_value = (
            lax.all_gather(w, ("dp", "tm"), axis=0, tiled=True)
            for w in (cross_query, cross_key, cross_value)
        )
    cross_width = cross_query.shape[1]
    rows, dim = frames.shape[1], frames.shape[2]
    width = out_w.shape[1]
    tokens = dec_states.shape[0] // MB

    bf, f32 = jnp.bfloat16, jnp.float32
    dma = pltpu.SemaphoreType.DMA
    vmem = pl.BlockSpec(memory_space=pltpu.VMEM)
    context, grad_t = pl.pallas_call(
        functools.partial(kernel, sizes, spread),
        out_shape=(
            jax.ShapeDtypeStruct((MB * tokens, cross_width), bf),
            jax.ShapeDtypeStruct((dim // group, cross_width), f32),
        ),
        in_specs=[vmem] * 10,
        out_specs=(vmem, vmem),
        scratch_shapes=[
            pltpu.VMEM((dim, 3 * width), bf),
            pltpu.VMEM((dim, width), bf),
            pltpu.VMEM((dim, 3 * cross_width), bf),
            pltpu.VMEM((MB, rows, rows + 2 * BLK), f32),
            pltpu.VMEM((MB, n_tm * tokens, rows), f32),
            pltpu.VMEM((group, MB * tokens, dim // group), bf),
            pltpu.VMEM((MB, rows, dim), bf),
            pltpu.VMEM((MB, rows, dim), bf),
            pltpu.VMEM((MB, rows + 2 * BLK, 2 * width), bf),
            pltpu.VMEM((MB, rows, dim), bf),
            pltpu.VMEM((n_tm, MB, tokens, cross_width), bf),
            pltpu.VMEM((MB, n_tm, tokens, 2 * cross_width), f32),
            pltpu.VMEM((n_tm, MB, tokens, 2 * cross_width), f32),
            pltpu.VMEM((group, MB * tokens, cross_width), bf),
            pltpu.VMEM((group, MB * tokens, dim // group), bf),
            dma((MB,)),
            dma((MB,)),
            dma((2, MB)),
            dma((2, MB)),
            dma((MB, rows // PIECE)),
            dma((MB, rows // PIECE)),
            dma((n_tm,)),
            dma((n_tm,)),
            dma((MB, n_tm)),
            dma((MB, n_tm)),
            dma((group,)),
            dma((group,)),
            dma((group,)),
            dma((group,)),
            dma((3, 14)),
            dma((3, 14)),
        ],
        compiler_params=pltpu.CompilerParams(
            collective_id=0, has_side_effects=True, vmem_limit_bytes=56 * 2**20
        ),
    )(frames, block_mask, span_segment, dec_states, cotangent, qkv_w, out_w, cross_query, cross_key, cross_value)
    return context, grad_t.T


def solution(mesh):
    sizes = tuple(mesh.shape[a] for a in ("dp", "section", "tm"))
    in_specs = (
        P("dp", "tm", None),
        P("dp", "tm", None),
        P("dp", None),
        P(("dp", "tm"), None),
        P("section", ("dp", "tm"), None),
        P("section", None, ("dp", "tm")),
        P(("dp", "tm"), "section"),
        P(("dp", "tm"), "section"),
        P(("dp", "tm"), "section"),
        P(("dp", "tm"), None),
    )
    out_specs = (P(("dp", "tm"), "section"), P("section", ("dp", "tm")))
    return jax.shard_map(
        functools.partial(per_device, sizes),
        mesh=mesh,
        in_specs=in_specs,
        out_specs=out_specs,
        check_vma=False,
    )
```
